512 devices in a mesh: az: 16 (over x, z_hi), ax: 32 (over z_lo, y, core).
Axes of the slice: x: 4, y: 4, z: 16 (z_hi: 4, z_lo: 4; z = z_hi * 4 + z_lo), core: 2. Of those that a mesh axis runs over, the one named last changes fastest.
Arguments:
- adj_coef: float32 [2, 512, 1024, 128], P(None, 'az', 'ax'), may hold values from -6 to 6
- grid_state: bfloat16 [2, 128, 512, 1024], P(None, 'az', 'ax'), may hold values from -4 to 4
- block_index: int32 [512, 1024], P('az', 'ax'), may hold values from 0 to 7
- frozen_depth: int32 [512, 1024], P('ax'), may hold values from 0 to 32
- inv_blocks: float32 [8, 2, 128, 128], replicated, may hold values from -1 to 2, as said below
Outputs:
- adj_prev: float32 [2, 512, 1024, 128], P(None, 'az', 'ax')
The draws below stay inside these ranges and needn't reach their ends.
Inputs may be any that keep to these rules, and one draw needn't show every extreme that they name: `inv_blocks`: each block is a dense matrix with a positive diagonal.
All inputs are finite; a program needn't handle non-finite values.
Results may differ from the reference program's by a relative error of at most 0.0003.
Values may be sent and summed in bfloat16 or wider, within the bound.
A program may use at most 128 MiB of HBM per device.

```python
import math
import jax
import jax.numpy as jnp
from jax import lax

FIELDS = 2
NT = 512
NZ = 1024
R = 128
NB = 8


def draw_inv_blocks(key, part):
    key = jax.random.fold_in(key, 7)
    key_diag, key_rest = jax.random.split(key)
    diagonal = jax.random.uniform(key_diag, (NB, FIELDS, R), jnp.float32, 0.5, 1.5)
    rest = jax.random.normal(key_rest, (NB, FIELDS, R, R), jnp.float32) * 0.3
    rest = jnp.clip(rest, -1.2, 1.2) / math.sqrt(R)
    identity = jnp.eye(R, dtype=jnp.float32)
    return diagonal[..., None] * identity + rest


def place_ends(entries, stream_key, low, largest):
    place = [jax.random.randint(jax.random.fold_in(stream_key, axis), (), 0, length) for axis, length in enumerate(entries.shape)]
    widest = entries.shape.index(max(entries.shape))
    neighbour = place[:widest] + [(place[widest] + 1) % entries.shape[widest]] + place[widest + 1:]
    return entries.at[tuple(place)].set(low).at[tuple(neighbour)].set(largest)


def block_scale(stream_key, dims, cuts, low, largest):
    def one(dim, parts):
        draws = jax.random.uniform(jax.random.fold_in(jax.random.fold_in(stream_key, 6), dim), (parts,), jnp.float32, low / len(cuts), largest / len(cuts))
        return jnp.repeat(jnp.exp(draws), dims[dim] // parts).reshape((-1,) + (1,) * (len(dims) - dim - 1))

    gain = one(*cuts[0])
    for cut in cuts[1:]:
        gain = gain * one(*cut)
    return gain


def bell_draw(own_key, shape, scale, most, cuts=(), kind=jnp.bfloat16):
    values = jax.random.normal(own_key, shape, jnp.float32) * scale
    if len(cuts) > 0:
        values = block_scale(own_key, shape, cuts, -0.22, 0.18) * values
    return jnp.clip(values, min=-most, max=most).astype(kind)


def setup_inputs(seed: int = 0) -> dict:
    streams_of = jax.random.split(jax.random.key(seed), 6)
    adj_coef = bell_draw(streams_of[0], (FIELDS, NT, NZ, R), 1.0, 6.0, ((1, 16), (2, 32)), jnp.float32)
    grid_state = bell_draw(streams_of[1], (FIELDS, R, NT, NZ), 1.0, 4.0, ((1, 16), (2, 32)))
    block_index = place_ends(jax.random.randint(streams_of[2], (NT, NZ), 0, NB), jax.random.fold_in(streams_of[2], 1), 0, NB - 1).astype(jnp.int32)
    frozen_depth = place_ends(jax.random.randint(streams_of[3], (NT, NZ), 0, R // 4 + 1), jax.random.fold_in(streams_of[3], 1), 0, (R // 4 + 1) - 1).astype(jnp.int32)
    inv_blocks = draw_inv_blocks(jax.random.fold_in(streams_of[5], 71), 0)
    return {"adj_coef": adj_coef, "grid_state": grid_state, "block_index": block_index, "frozen_depth": frozen_depth, "inv_blocks": inv_blocks}


penalty = 2.0
step_dt = 0.3

def hartley(count):
    index = jnp.arange(count, dtype=jnp.int32)
    product = index[:, None] * index[None, :] % count
    angle = product.astype(jnp.float32) * (2.0 * math.pi / count)
    return (jnp.cos(angle) + jnp.sin(angle)) / math.sqrt(count)

def chebyshev(count):
    index = jnp.arange(count, dtype=jnp.int32)
    product = index[:, None] * index[None, :] % (2 * (count - 1))
    angle = product.astype(jnp.float32) * (math.pi / (count - 1))
    return jnp.cos(angle) * math.sqrt(2.0 / count)

def reference(adj_coef, grid_state, block_index, frozen_depth, inv_blocks):
    high = lax.Precision.HIGHEST
    adj_implicit = jnp.zeros_like(adj_coef)
    for block in range(NB):
        product = jnp.einsum('ftzn,fmn->ftzm', adj_coef, inv_blocks[block], precision=high)
        chosen = (block_index == block)[None, :, :, None]
        adj_implicit = adj_implicit + jnp.where(chosen, product, jnp.zeros_like(product))
    radial_table = chebyshev(R)
    theta_table = hartley(NT)
    axial_table = hartley(NZ)
    radial_grid = jnp.einsum('ftzn,in->ftzi', adj_implicit, radial_table, precision=high)
    theta_grid = jnp.einsum('ftzi,jt->fjzi', radial_grid, theta_table, precision=high)
    adj_grid = jnp.einsum('fjzi,wz->fijw', theta_grid, axial_table, precision=high)
    state = grid_state.astype(jnp.float32)
    speed_sq = lax.optimization_barrier(jnp.sum(state * state, axis=0))
    viscosity = (1.0 + speed_sq) ** (-0.25)
    tangent = 0.5 * (1.0 + speed_sq) ** (-1.25)
    radius_idx = jnp.arange(R, dtype=jnp.int32)
    frozen = (radius_idx[:, None, None] >= R - frozen_depth[None, :, :]).astype(jnp.float32)
    coupling = lax.optimization_barrier(jnp.sum(state * adj_grid, axis=0))
    forced = -(viscosity + penalty * frozen)[None] * adj_grid + (tangent * coupling)[None] * state
    axial_back = jnp.einsum('fijw,wz->fjzi', forced, axial_table, precision=high)
    theta_back = jnp.einsum('fjzi,jt->ftzi', axial_back, theta_table, precision=high)
    gamma = jnp.einsum('ftzi,in->ftzn', theta_back, radial_table, precision=high)
    return adj_implicit + step_dt * gamma
```

```python
import math

import jax
import jax.numpy as jnp
import ml_dtypes
import numpy as np
from jax import lax
from jax.experimental import pallas as pl
from jax.experimental.pallas import tpu as pltpu
from jax.sharding import PartitionSpec as P

NT = 512
NZ = 1024
R = 128
NB = 8
penalty = 2.0
step_dt = 0.3
QMAX = 32767.0
F32 = jnp.float32
BF16 = jnp.bfloat16
I16 = jnp.int16
MESH = pl.DeviceIdType.MESH


def hartley(count):
    index = np.arange(count, dtype=np.int64)
    angle = (index[:, None] * index[None, :] % count) * (2.0 * math.pi / count)
    return (np.cos(angle) + np.sin(angle)) / math.sqrt(count)


def chebyshev(count):
    index = np.arange(count, dtype=np.int64)
    angle = (index[:, None] * index[None, :] % (2 * (count - 1))) * (math.pi / (count - 1))
    return np.cos(angle) * math.sqrt(2.0 / count)


def parts(table):
    high = table.astype(ml_dtypes.bfloat16)
    low = (table - high.astype(np.float64)).astype(ml_dtypes.bfloat16)
    return high, low


def tables():
    q, zl, i = np.meshgrid(np.arange(8), np.arange(4), np.arange(16), indexing="ij")
    theta_order = (16 * (zl * 8 + q) + i).reshape(-1)
    az, t4, tg = np.meshgrid(np.arange(16), np.arange(4), np.arange(8), indexing="ij")
    mode_order = (32 * az + tg * 4 + t4).reshape(-1)
    q, zl, i = np.meshgrid(np.arange(8), np.arange(4), np.arange(32), indexing="ij")
    axial_order = (32 * (zl * 8 + q) + i).reshape(-1)
    theta = hartley(NT)[theta_order][:, mode_order]
    axial = hartley(NZ)[axial_order]
    radial = chebyshev(R)
    ch, cl = parts(radial)
    th, tl = parts(theta)
    bh, bl = parts(theta.T)
    wh, wl = parts(axial)
    vh, vl = parts(axial.T)
    return [
        np.concatenate([ch, ch, cl], axis=1),
        np.concatenate([ch, ch, cl], axis=0),
        np.concatenate([th, th, tl], axis=1),
        np.concatenate([bh, bh, bl], axis=1),
        wh,
        wl,
        np.ascontiguousarray(vh),
        np.ascontiguousarray(vl),
    ]


def split(value):
    high = value.astype(BF16)
    low = (value - high.astype(F32)).astype(BF16)
    return high, low


def dot(a, b, dims=((1,), (0,))):
    return lax.dot_general(a, b, (dims, ((), ())), preferred_element_type=F32)


def swap_groups(tiles):
    lane = lax.broadcasted_iota(jnp.int32, tiles[0].shape, 1)
    first = lane < 64
    even = lane % 64 < 32
    t0, t1, t2, t3 = tiles
    a0 = jnp.where(first, t0, pltpu.roll(t2, 64, 1))
    a2 = jnp.where(first, pltpu.roll(t0, 64, 1), t2)
    a1 = jnp.where(first, t1, pltpu.roll(t3, 64, 1))
    a3 = jnp.where(first, pltpu.roll(t1, 64, 1), t3)
    b0 = jnp.where(even, a0, pltpu.roll(a1, 32, 1))
    b1 = jnp.where(even, pltpu.roll(a0, 96, 1), a1)
    b2 = jnp.where(even, a2, pltpu.roll(a3, 32, 1))
    b3 = jnp.where(even, pltpu.roll(a2, 96, 1), a3)
    return [b0, b1, b2, b3]


def quantize(value, inverse):
    return jnp.round(value * inverse).astype(jnp.int32).astype(I16)


def restore(value, scale):
    return value.astype(jnp.int32).astype(F32) * scale


def kernel(
    x_ref, st_ref, bi_ref, fd_ref, inv_ref, cf_ref, cb_ref,
    tf_in, tb_in, wh_in, wl_in, vh_in, vl_in,
    out_ref,
    tf_ref, tb_ref, wh_ref, wl_ref, vh_ref, vl_ref,
    wc_ref, impl_ref, s32_ref, d32_ref, b32_ref,
    s16_ref, xb_ref, zb_ref, sc_ref, xsc_ref, zsc_ref,
    ysend_ref, yrecv_ref, ysc_ref, yscr_ref,
    state_ref, fd16_ref, fdall_ref, keep_ref, tang_ref,
    xcat_ref, a_ref, f_ref,
    table_sem, xs_sem, xr_sem, zs_sem, zr_sem, ys_sem, yr_sem,
    xcs_sem, xcr_sem, zcs_sem, zcr_sem, ycs_sem, ycr_sem,
    us_sem, ur_sem, fs_sem, fr_sem, own_sem,
):
    az = lax.axis_index("az")
    ax = lax.axis_index("ax")
    x = az // 4
    zl = ax // 8
    q = ax % 8
    z = (az % 4) * 4 + zl
    group = x * 16 + z

    def at_xz(xx, zz):
        return (xx * 4 + zz // 4, (zz % 4) * 8 + q)

    def at_q(qq):
        return (az, zl * 8 + qq)

    def remote(src, dst, send, recv, device):
        return pltpu.make_async_remote_copy(
            src_ref=src, dst_ref=dst, send_sem=send, recv_sem=recv, device_id=device, device_id_type=MESH
        )

    table_copies = [
        pltpu.make_async_copy(src, dst, table_sem.at[n])
        for n, (src, dst) in enumerate(
            [(tf_in, tf_ref), (tb_in, tb_ref), (wh_in, wh_ref), (wl_in, wl_ref), (vh_in, vh_ref), (vl_in, vl_ref)]
        )
    ]
    for copy in table_copies:
        copy.start()
    barrier = pltpu.get_barrier_semaphore()
    for k in range(1, 4):
        pl.semaphore_signal(barrier, inc=1, device_id=at_xz((x + k) % 4, z), device_id_type=MESH)
    for k in range(1, 16):
        pl.semaphore_signal(barrier, inc=1, device_id=at_xz(x, (z + k) % 16), device_id_type=MESH)
    for k in range(1, 8):
        pl.semaphore_signal(barrier, inc=1, device_id=at_q((q + k) % 8), device_id_type=MESH)

    def x_copies(leg, rho, k, to, frm):
        return [
            remote(s16_ref.at[leg, rho, to], xb_ref.at[leg, rho, frm], xs_sem.at[leg, rho, k], xr_sem.at[leg, rho, k], at_xz(to, z)),
            remote(sc_ref.at[leg, rho], xsc_ref.at[leg, rho, frm], xcs_sem.at[leg, rho, k], xcr_sem.at[leg, rho, k], at_xz(to, z)),
        ]

    def z_copies(leg, rho, k, to, frm):
        return [
            remote(xb_ref.at[leg, rho, :, to], zb_ref.at[leg, rho, frm], zs_sem.at[leg, rho, k], zr_sem.at[leg, rho, k], at_xz(x, to)),
            remote(xsc_ref.at[leg, rho], zsc_ref.at[leg, rho, frm], zcs_sem.at[leg, rho, k], zcr_sem.at[leg, rho, k], at_xz(x, to)),
        ]

    def y_copies(leg, rho, k, to, frm):
        return [
            remote(ysend_ref.at[leg, rho, to], yrecv_ref.at[leg, rho, frm], ys_sem.at[leg, rho, k], yr_sem.at[leg, rho, k], at_q(to)),
            remote(ysc_ref.at[leg, rho, to], yscr_ref.at[leg, rho, frm], ycs_sem.at[leg, rho, k], ycr_sem.at[leg, rho, k], at_q(to)),
        ]

    def exchange(copies, me, count):
        def start(leg, rho):
            order = sorted(range(1, count), key=lambda k: (-min(k, count - k), k))
            for k in order:
                for copy in copies(leg, rho, k, (me + k) % count, me):
                    copy.start()

        def arrive(leg, rho):
            for k in range(1, count):
                frm = (me + count - k) % count
                for copy in copies(leg, rho, k, me, frm):
                    copy.wait_recv()

        def sent(leg, rho):
            for k in range(1, count):
                for copy in copies(leg, rho, k, (me + k) % count, me):
                    copy.wait_send()

        return start, arrive, sent

    x_start, x_arrive, x_sent = exchange(x_copies, x, 4)
    z_start, z_arrive, z_sent = exchange(z_copies, z, 16)
    y_start, y_arrive, y_sent = exchange(y_copies, q, 8)

    def x_phase(leg, rho):
        x_start(leg, rho)
        xb_ref[leg, rho, x] = s16_ref[leg, rho, x]
        xsc_ref[leg, rho, x] = sc_ref[leg, rho]

    def z_phase(leg, rho):
        x_arrive(leg, rho)
        z_start(leg, rho)
        zb_ref[leg, rho, z] = xb_ref[leg, rho, :, z]
        zsc_ref[leg, rho, z] = xsc_ref[leg, rho]

    def y_phase(leg, rho):
        y_start(leg, rho)
        yrecv_ref[leg, rho, q] = ysend_ref[leg, rho, q]
        yscr_ref[leg, rho, q] = ysc_ref[leg, rho, q]

    def radial_forward(f):
        for b in range(NB):
            high, low = split(inv_ref[b, f].T)
            wc_ref[b * 384 : b * 384 + 128] = high
            wc_ref[b * 384 + 128 : b * 384 + 256] = high
            wc_ref[b * 384 + 256 : b * 384 + 384] = low
        eye = lax.broadcasted_iota(jnp.int32, (32, 32), 0) == lax.broadcasted_iota(jnp.int32, (32, 32), 1)
        ones = jnp.ones((32, 128), BF16)
        largest = jnp.zeros((1, 128), F32)
        for rt in range(4):
            rows = slice(rt * 256, rt * 256 + 256)
            labels = bi_ref[rt * 8 : rt * 8 + 8, :].astype(F32)
            spread = [jnp.where(eye, jnp.broadcast_to(labels[t : t + 1], (32, 32)), 0.0) for t in range(8)]
            label = dot(jnp.concatenate(spread, axis=0).astype(BF16), ones)
            high, low = split(x_ref[f, rows, :])
            total = jnp.zeros((256, 128), F32)
            for b in range(0, NB, 2):
                pieces = []
                for c in (b, b + 1):
                    mask = jnp.where(label == float(c), 1.0, 0.0).astype(BF16)
                    kept = high * mask
                    pieces += [kept, low * mask, kept]
                total += dot(jnp.concatenate(pieces, axis=1), wc_ref[b * 384 : b * 384 + 768, :])
            impl_ref[f, rows, :] = total
            high, low = split(total)
            grid = dot(cf_ref[...], jnp.concatenate([high, low, high], axis=1), ((1,), (1,)))
            for h in range(2):
                piece = grid[:, h * 128 : h * 128 + 128]
                s32_ref[f, pl.ds(rt * 2 + h, 128, stride=8), :] = piece
                largest = jnp.maximum(largest, jnp.max(jnp.abs(piece), axis=0, keepdims=True))
        return largest

    def quantize_forward(rho, inverse):
        def body(g, carry):
            base = pl.multiple_of(g * 16 + rho * 8, 8)
            both = jnp.concatenate([s32_ref[f, pl.ds(base, 8), :] for f in range(2)], axis=0)
            s16_ref[0, rho, g // 16, g % 16] = quantize(both, inverse)
            return carry

        lax.fori_loop(0, 64, body, 0)

    largest = radial_forward(0)

    pl.semaphore_wait(barrier, 25)

    fd16_ref[...] = fd_ref[...].astype(I16)

    def state_copies(k, to, frm):
        home = (az, to * 8 + q)
        return [
            remote(st_ref.at[:, pl.ds(2 * to, 2)], state_ref.at[frm], us_sem.at[k], ur_sem.at[k], home),
            remote(fd16_ref, fdall_ref.at[frm], fs_sem.at[k], fr_sem.at[k], home),
        ]

    for k in range(1, 4):
        for copy in state_copies(k, (zl + k) % 4, zl):
            copy.start()
    own_state = pltpu.make_async_copy(st_ref.at[:, pl.ds(2 * zl, 2)], state_ref.at[zl], own_sem)
    own_state.start()
    fdall_ref[zl] = fd16_ref[...]

    largest = jnp.maximum(jnp.maximum(largest, radial_forward(1)), 1e-30)
    inverse = QMAX / largest
    for rho in range(2):
        sc_ref[0, rho] = largest * (1.0 / QMAX)
        quantize_forward(rho, inverse)
        x_phase(0, rho)
    for rho in range(2):
        z_phase(0, rho)

    for k in range(1, 4):
        for copy in state_copies(k, zl, (zl + 4 - k) % 4):
            copy.wait_recv()
    own_state.wait()
    for rho in range(2):
        for s in range(4):
            u0 = state_ref[s, 0, rho].astype(F32)
            u1 = state_ref[s, 1, rho].astype(F32)
            root = lax.rsqrt(1.0 + (u0 * u0 + u1 * u1))
            viscosity = root * lax.rsqrt(root)
            depth = fdall_ref[s].astype(jnp.int32)
            frozen = jnp.where(2 * group + rho >= R - depth, penalty, 0.0)
            keep_ref[rho, s * 16 : s * 16 + 16] = viscosity + frozen
            tang_ref[rho, s * 16 : s * 16 + 16] = 0.5 * viscosity * (root * root)
    for copy in table_copies:
        copy.wait()

    def theta_product(table_ref):
        return dot(table_ref[...], xcat_ref[...])

    def keep_columns(rows, f, value):
        high, low = split(value)
        start, size = rows
        columns = slice(f * 128, f * 128 + 128)
        xcat_ref[pl.ds(start, size), columns] = high
        xcat_ref[pl.ds(512 + start, size), columns] = low
        xcat_ref[pl.ds(1024 + start, size), columns] = high

    def theta_forward(rho):
        z_arrive(0, rho)

        def body(n, carry):
            zh = n % 4
            xx = n // 4
            tiles = [
                restore(zb_ref[0, rho, zh * 4 + s, xx], zsc_ref[0, rho, zh * 4 + s, xx]) for s in range(4)
            ]
            tiles = swap_groups(tiles)
            for f in range(2):
                rows = jnp.concatenate([tile[f * 8 : f * 8 + 8] for tile in tiles], axis=0)
                keep_columns((pl.multiple_of(n * 32, 32), 32), f, rows)
            return carry

        lax.fori_loop(0, 16, body, 0)
        grid = theta_product(tf_ref)
        most = jnp.max(jnp.abs(grid), axis=0, keepdims=True)
        most = jnp.maximum(jnp.maximum(most[:, :128], most[:, 128:]), 1e-30)
        inverse = QMAX / most
        scale = most * (1.0 / QMAX)
        for p in range(8):
            ysc_ref[0, rho, p] = scale
            for f in range(2):
                ysend_ref[0, rho, p, f] = quantize(grid[p * 64 : p * 64 + 64, f * 128 : f * 128 + 128], inverse)
        y_phase(0, rho)

    def axial_both(rho):
        y_arrive(0, rho)
        for p in range(8):
            for f in range(2):
                high, low = split(restore(yrecv_ref[0, rho, p, f], yscr_ref[0, rho, p]))
                a_ref[f * 64 : f * 64 + 64, p * 128 : p * 128 + 128] = high
                a_ref[128 + f * 64 : 128 + f * 64 + 64, p * 128 : p * 128 + 128] = low
        for n in range(4):
            columns = slice(n * 256, n * 256 + 256)
            twice = dot(a_ref[...], wh_ref[:, columns])
            grid = twice[:128] + twice[128:] + dot(a_ref[:128], wl_ref[:, columns])
            keep = keep_ref[rho, :, columns]
            u0 = jnp.concatenate([state_ref[s, 0, rho, :, columns] for s in range(4)], axis=0).astype(F32)
            u1 = jnp.concatenate([state_ref[s, 1, rho, :, columns] for s in range(4)], axis=0).astype(F32)
            g0 = grid[:64]
            g1 = grid[64:]
            pull = tang_ref[rho, :, columns] * (u0 * g0 + u1 * g1)
            for f, (u, g) in enumerate(((u0, g0), (u1, g1))):
                high, low = split(pull * u - keep * g)
                f_ref[f * 64 : f * 64 + 64, columns] = high
                f_ref[128 + f * 64 : 128 + f * 64 + 64, columns] = low
        for n in range(4):
            columns = slice(n * 256, n * 256 + 256)
            twice = dot(f_ref[...], vh_ref[:, columns])
            modes = twice[:128] + twice[128:] + dot(f_ref[:128], vl_ref[:, columns])
            most = jnp.maximum(jnp.max(jnp.abs(modes), axis=0, keepdims=True), 1e-30)
            inverse = QMAX / most
            scale = most * (1.0 / QMAX)
            for h in range(2):
                lanes = slice(h * 128, h * 128 + 128)
                ysc_ref[1, rho, 2 * n + h] = scale[:, lanes]
                for f in range(2):
                    ysend_ref[1, rho, 2 * n + h, f] = quantize(modes[f * 64 : f * 64 + 64, lanes], inverse[:, lanes])
        y_phase(1, rho)

    def theta_back(rho):
        y_arrive(1, rho)
        for p in range(8):
            for f in range(2):
                keep_columns((p * 64, 64), f, restore(yrecv_ref[1, rho, p, f], yscr_ref[1, rho, p]))
        modes = theta_product(tb_ref)
        most = jnp.zeros((16, 128), F32)
        for n in range(16):
            tiles = [
                jnp.concatenate(
                    [modes[n * 32 + a * 8 : n * 32 + a * 8 + 8, f * 128 : f * 128 + 128] for f in range(2)], axis=0
                )
                for a in range(4)
            ]
            tiles = swap_groups(tiles)
            for s in range(4):
                b32_ref[n * 4 + s] = tiles[s]
                most = jnp.maximum(most, jnp.abs(tiles[s]))
        most = jnp.maximum(jnp.max(most, axis=0, keepdims=True), 1e-30)
        inverse = QMAX / most
        sc_ref[1, rho] = most * (1.0 / QMAX)

        def body(g, carry):
            s16_ref[1, rho, g // 16, g % 16] = quantize(b32_ref[g], inverse)
            return carry

        lax.fori_loop(0, 64, body, 0)
        x_phase(1, rho)

    theta_forward(0)
    axial_both(0)
    theta_back(0)
    theta_forward(1)
    z_phase(1, 0)
    axial_both(1)
    theta_back(1)
    z_phase(1, 1)

    for rho in range(2):
        z_arrive(1, rho)

        def body(g, carry):
            tile = restore(zb_ref[1, rho, g % 16, g // 16], zsc_ref[1, rho, g % 16, g // 16])
            base = pl.multiple_of(g * 16 + rho * 8, 8)
            for f in range(2):
                d32_ref[f, pl.ds(base, 8), :] = tile[f * 8 : f * 8 + 8]
            return carry

        lax.fori_loop(0, 64, body, 0)
    for f in range(2):
        for tg in range(8):
            high, low = split(d32_ref[f, pl.ds(tg, 128, stride=8), :])
            gamma = dot(jnp.concatenate([high, low, high], axis=0), cb_ref[...], ((0,), (0,)))
            rows = slice(tg * 128, tg * 128 + 128)
            out_ref[f, rows, :] = impl_ref[f, rows, :] + step_dt * gamma

    for leg in range(2):
        for rho in range(2):
            x_sent(leg, rho)
            z_sent(leg, rho)
            y_sent(leg, rho)
    for k in range(1, 4):
        for copy in state_copies(k, (zl + k) % 4, zl):
            copy.wait_send()


def on_device(adj_coef, grid_state, block_index, frozen_depth, inv_blocks):
    constants = [jnp.asarray(table) for table in tables()]
    vmem = pl.BlockSpec(memory_space=pltpu.VMEM)
    hbm = pl.BlockSpec(memory_space=pl.ANY)
    dma = pltpu.SemaphoreType.DMA
    scratch = [
        pltpu.VMEM((512, 1536), BF16),
        pltpu.VMEM((512, 1536), BF16),
        pltpu.VMEM((NZ, NZ), BF16),
        pltpu.VMEM((NZ, NZ), BF16),
        pltpu.VMEM((NZ, NZ), BF16),
        pltpu.VMEM((NZ, NZ), BF16),
        pltpu.VMEM((NB * 384, 128), BF16),
        pltpu.VMEM((2, 1024, 128), F32),
        pltpu.VMEM((2, 1024, 128), F32),
        pltpu.VMEM((2, 1024, 128), F32),
        pltpu.VMEM((64, 16, 128), F32),
        pltpu.VMEM((2, 2, 4, 16, 16, 128), I16),
        pltpu.VMEM((2, 2, 4, 16, 16, 128), I16),
        pltpu.VMEM((2, 2, 16, 4, 16, 128), I16),
        pltpu.VMEM((2, 2, 1, 128), F32),
        pltpu.VMEM((2, 2, 4, 1, 128), F32),
        pltpu.VMEM((2, 2, 16, 4, 1, 128), F32),
        pltpu.VMEM((2, 2, 8, 2, 64, 128), I16),
        pltpu.VMEM((2, 2, 8, 2, 64, 128), I16),
        pltpu.VMEM((2, 2, 8, 1, 128), F32),
        pltpu.VMEM((2, 2, 8, 1, 128), F32),
        pltpu.VMEM((4, 2, 2, 16, NZ), BF16),
        pltpu.VMEM((16, NZ), I16),
        pltpu.VMEM((4, 16, NZ), I16),
        pltpu.VMEM((2, 64, NZ), F32),
        pltpu.VMEM((2, 64, NZ), F32),
        pltpu.VMEM((1536, 256), BF16),
        pltpu.VMEM((256, NZ), BF16),
        pltpu.VMEM((256, NZ), BF16),
        dma((6,)),
        dma((2, 2, 4)), dma((2, 2, 4)), dma((2, 2, 16)), dma((2, 2, 16)), dma((2, 2, 8)), dma((2, 2, 8)),
        dma((2, 2, 4)), dma((2, 2, 4)), dma((2, 2, 16)), dma((2, 2, 16)), dma((2, 2, 8)), dma((2, 2, 8)),
        dma((4,)), dma((4,)), dma((4,)), dma((4,)), dma,
    ]
    step = pl.pallas_call(
        kernel,
        out_shape=jax.ShapeDtypeStruct((2, 1024, R), F32),
        in_specs=[vmem, hbm, vmem, vmem, vmem, vmem, vmem] + [hbm] * 6,
        out_specs=vmem,
        scratch_shapes=scratch,
        compiler_params=pltpu.CompilerParams(
            collective_id=0, has_side_effects=True, vmem_limit_bytes=48 * 1024 * 1024
        ),
    )
    flat = adj_coef.reshape(2, 1024, R)
    result = step(flat, grid_state, block_index, frozen_depth, inv_blocks, *constants)
    return result.reshape(2, 32, 32, R)


def solution(mesh):
    placed = (
        P(None, "az", "ax", None),
        P(None, "az", "ax", None),
        P("az", "ax"),
        P("ax", None),
        P(),
    )
    return jax.shard_map(
        on_device, mesh=mesh, in_specs=placed, out_specs=P(None, "az", "ax", None), check_vma=False
    )
```

```python
import math

import jax
import jax.numpy as jnp
import ml_dtypes
import numpy as np
from jax import lax
from jax.experimental import pallas as pl
from jax.experimental.pallas import tpu as pltpu
from jax.sharding import PartitionSpec as P

NT = 512
NZ = 1024
R = 128
NB = 8
penalty = 2.0
step_dt = 0.3
QMAX = 32767.0
ROUNDER = 12582912.0
F32 = jnp.float32
BF16 = jnp.bfloat16
I16 = jnp.int16
MESH = pl.DeviceIdType.MESH


def hartley(count):
    index = np.arange(count, dtype=np.int64)
    angle = (index[:, None] * index[None, :] % count) * (2.0 * math.pi / count)
    return (np.cos(angle) + np.sin(angle)) / math.sqrt(count)


def chebyshev(count):
    index = np.arange(count, dtype=np.int64)
    angle = (index[:, None] * index[None, :] % (2 * (count - 1))) * (math.pi / (count - 1))
    return np.cos(angle) * math.sqrt(2.0 / count)


def parts(table):
    high = table.astype(ml_dtypes.bfloat16)
    low = (table - high.astype(np.float64)).astype(ml_dtypes.bfloat16)
    return high, low


def tables():
    q, zl, i = np.meshgrid(np.arange(8), np.arange(4), np.arange(16), indexing="ij")
    theta_order = (16 * (zl * 8 + q) + i).reshape(-1)
    az, t4, tg = np.meshgrid(np.arange(16), np.arange(4), np.arange(8), indexing="ij")
    mode_order = (32 * az + tg * 4 + t4).reshape(-1)
    q, zl, i = np.meshgrid(np.arange(8), np.arange(4), np.arange(32), indexing="ij")
    axial_order = (32 * (zl * 8 + q) + i).reshape(-1)
    theta = hartley(NT)[theta_order][:, mode_order]
    axial = hartley(NZ)[axial_order]
    radial = chebyshev(R)
    ch, cl = parts(radial)
    dh, dl = parts(np.stack([radial[0::2], radial[1::2]]))
    th, tl = parts(theta)
    bh, bl = parts(theta.T)
    wh, wl = parts(axial)
    vh, vl = parts(axial.T)
    return [
        np.concatenate([ch, ch, cl], axis=1),
        np.stack([np.concatenate([dh[i], dh[i], dl[i]], axis=0) for i in range(2)]),
        np.concatenate([th, th, tl], axis=1),
        np.concatenate([bh, bh, bl], axis=1),
        wh,
        wl,
        np.ascontiguousarray(vh),
        np.ascontiguousarray(vl),
    ]


def split(value):
    high = value.astype(BF16)
    low = (value - high.astype(F32)).astype(BF16)
    return high, low


def dot(a, b, dims=((1,), (0,))):
    return lax.dot_general(a, b, (dims, ((), ())), preferred_element_type=F32)


def swap_groups(tiles):
    lane = lax.broadcasted_iota(jnp.int32, tiles[0].shape, 1)
    first = lane < 64
    even = lane % 64 < 32
    t0, t1, t2, t3 = tiles
    a0 = jnp.where(first, t0, pltpu.roll(t2, 64, 1))
    a2 = jnp.where(first, pltpu.roll(t0, 64, 1), t2)
    a1 = jnp.where(first, t1, pltpu.roll(t3, 64, 1))
    a3 = jnp.where(first, pltpu.roll(t1, 64, 1), t3)
    b0 = jnp.where(even, a0, pltpu.roll(a1, 32, 1))
    b1 = jnp.where(even, pltpu.roll(a0, 96, 1), a1)
    b2 = jnp.where(even, a2, pltpu.roll(a3, 32, 1))
    b3 = jnp.where(even, pltpu.roll(a2, 96, 1), a3)
    return [b0, b1, b2, b3]


def quantize(value, inverse):
    whole = (value * inverse + ROUNDER) - ROUNDER
    return whole.astype(jnp.int32).astype(I16)


def restore(value, scale):
    return value.astype(jnp.int32).astype(F32) * scale


def kernel(
    x_in, st_ref, bi_ref, fd_ref, inv_in, cf_ref, cb_ref,
    tf_in, tb_in, wh_in, wl_in, vh_in, vl_in,
    out_ref,
    x_ref, inv_ref, tf_ref, tb_ref, wh_ref, wl_ref, vh_ref, vl_ref,
    wc_ref, impl_ref, s32_ref, d32_ref,
    s16_ref, xb_ref, zb_ref, sc_ref, xsc_ref, zsc_ref,
    ysend_ref, yrecv_ref, ysc_ref, yscr_ref,
    state_ref, fd16_ref, fdall_ref, keep_ref, tang_ref,
    xcat_ref, a_ref, f_ref,
    table_sem, xs_sem, xr_sem, zs_sem, zr_sem, ys_sem, yr_sem,
    xcs_sem, xcr_sem, zcs_sem, zcr_sem, ycs_sem, ycr_sem,
    us_sem, ur_sem, fs_sem, fr_sem, gs_sem, gr_sem, own_sem,
):
    az = lax.axis_index("az")
    ax = lax.axis_index("ax")
    x = lax.div(az, 4)
    zl = lax.div(ax, 8)
    q = lax.rem(ax, 8)
    y = lax.div(q, 2)
    core = lax.rem(q, 2)
    z = lax.rem(az, 4) * 4 + zl
    group = x * 16 + z

    x_to = [lax.rem(x + k, 4) for k in range(4)]
    z_to = [lax.rem(z + k, 16) for k in range(16)]
    x_home = [(xx * 4 + lax.rem(az, 4), ax) for xx in x_to]
    z_home = [(x * 4 + lax.div(zz, 4), lax.rem(zz, 4) * 8 + q) for zz in z_to]
    y_to = [lax.rem(y + k, 4) for k in range(4)]
    l_to = [lax.rem(zl + k, 4) for k in range(4)]
    l_home = [(az, ll * 8 + q) for ll in l_to]

    def y_home(k, h):
        return (az, zl * 8 + y_to[k] * 2 + h)

    def remote(src, dst, send, recv, device):
        return pltpu.make_async_remote_copy(
            src_ref=src, dst_ref=dst, send_sem=send, recv_sem=recv, device_id=device, device_id_type=MESH
        )

    table_copies = [
        pltpu.make_async_copy(src, dst, table_sem.at[n])
        for n, (src, dst) in enumerate(
            [
                (inv_in, inv_ref), (x_in, x_ref), (tf_in, tf_ref), (tb_in, tb_ref),
                (wh_in, wh_ref), (wl_in, wl_ref), (vh_in, vh_ref), (vl_in, vl_ref),
            ]
        )
    ]
    for copy in table_copies:
        copy.start()
    barrier = pltpu.get_barrier_semaphore()
    homes = x_home[1:] + z_home[1:] + [y_home(k, h) for k in range(1, 4) for h in range(2)] + [y_home(0, 1 - core)]
    for home in homes:
        pl.semaphore_signal(barrier, inc=1, device_id=home, device_id_type=MESH)

    def x_copies(leg, rho, k, to, frm, home):
        data = [
            remote(s16_ref.at[leg, rho, to], xb_ref.at[leg, rho, frm], xs_sem.at[leg, rho, k], xr_sem.at[leg, rho, k], home),
        ]
        if leg == 0 and rho == 1:
            return data
        return data + [
            remote(sc_ref.at[leg, rho, to], xsc_ref.at[leg, rho, frm], xcs_sem.at[leg, rho, k], xcr_sem.at[leg, rho, k], home),
        ]

    def z_copies(leg, rho, k, to, frm, home):
        data = [
            remote(xb_ref.at[leg, rho, :, to], zb_ref.at[leg, rho, frm], zs_sem.at[leg, rho, k], zr_sem.at[leg, rho, k], home),
        ]
        if leg == 0 and rho == 1:
            return data
        return data + [
            remote(xsc_ref.at[leg, rho], zsc_ref.at[leg, rho, frm], zcs_sem.at[leg, rho, k], zcr_sem.at[leg, rho, k], home),
        ]

    def exchange(copies, place, homes, count):
        def start(leg, rho):
            order = sorted(range(1, count), key=lambda k: (-min(k, count - k), k))
            for k in order:
                for copy in copies(leg, rho, k, place[k], place[0], homes[k]):
                    copy.start()

        def arrive(leg, rho):
            for k in range(1, count):
                for copy in copies(leg, rho, k, place[0], place[count - k], homes[k]):
                    copy.wait_recv()

        def sent(leg, rho):
            for k in range(1, count):
                for copy in copies(leg, rho, k, place[k], place[0], homes[k]):
                    copy.wait_send()

        return start, arrive, sent

    _, x_arrive, x_sent = exchange(x_copies, x_to, x_home, 4)
    z_start, z_arrive, z_sent = exchange(z_copies, z_to, z_home, 16)

    def y_copies(leg, rho, k, h, frm, frm_core):
        to = y_to[k] * 2 + h
        send = 2 * k + h
        recv = 2 * k + frm_core
        return [
            remote(ysend_ref.at[leg, rho, to], yrecv_ref.at[leg, rho, frm], ys_sem.at[leg, rho, send], yr_sem.at[leg, rho, recv], y_home(k, h)),
            remote(ysc_ref.at[leg, rho, to], yscr_ref.at[leg, rho, frm], ycs_sem.at[leg, rho, send], ycr_sem.at[leg, rho, recv], y_home(k, h)),
        ]

    def y_partners(k):
        return (0, 1) if k else (1 - core,)

    def y_send(leg, rho, k):
        for h in y_partners(k):
            for copy in y_copies(leg, rho, k, h, q, core):
                copy.start()
        if k == 0:
            yrecv_ref[leg, rho, q] = ysend_ref[leg, rho, q]
            yscr_ref[leg, rho, q] = ysc_ref[leg, rho, q]

    def y_arrive(leg, rho):
        for k in (2, 1, 3, 0):
            for h in y_partners(k):
                for copy in y_copies(leg, rho, k, core, y_to[(4 - k) % 4] * 2 + h, h):
                    copy.wait_recv()

    def y_sent(leg, rho):
        for k in range(4):
            for h in y_partners(k):
                for copy in y_copies(leg, rho, k, h, q, core):
                    copy.wait_send()

    def x_send(leg, rho, k):
        if k:
            for copy in x_copies(leg, rho, k, x_to[k], x, x_home[k]):
                copy.start()
        else:
            xb_ref[leg, rho, x] = s16_ref[leg, rho, x]
            if leg == 1 or rho == 0:
                xsc_ref[leg, rho, x] = sc_ref[leg, rho, x]

    def z_phase(leg, rho):
        x_arrive(leg, rho)
        z_start(leg, rho)
        zb_ref[leg, rho, z] = xb_ref[leg, rho, :, z]
        if leg == 1 or rho == 0:
            zsc_ref[leg, rho, z] = xsc_ref[leg, rho]

    def operators(f):
        for b in range(NB):
            high, low = split(inv_ref[b, f].T)
            columns = slice(b % 2 * 128, b % 2 * 128 + 128)
            wc_ref[f, b // 2, 0:128, columns] = high
            wc_ref[f, b // 2, 128:256, columns] = high
            wc_ref[f, b // 2, 256:384, columns] = low

    def radial_forward(f):
        eye = lax.broadcasted_iota(jnp.int32, (32, 32), 0) == lax.broadcasted_iota(jnp.int32, (32, 32), 1)
        ones = jnp.ones((32, 128), BF16)
        largest = jnp.zeros((4, 128), F32)
        for rt in range(4):
            rows = slice(rt * 256, rt * 256 + 256)
            labels = bi_ref[rt * 8 : rt * 8 + 8, :].astype(F32)
            spread = [jnp.where(eye, jnp.broadcast_to(labels[t : t + 1], (32, 32)), 0.0) for t in range(8)]
            label = dot(jnp.concatenate(spread, axis=0).astype(BF16), ones)
            high, low = split(x_ref[f, rows, :])
            both = jnp.concatenate([high, low, high], axis=1)
            total = jnp.zeros((256, 128), F32)
            for b in range(0, NB, 2):
                pair = dot(both, wc_ref[f, b // 2])
                total = jnp.where(label == float(b), pair[:, :128], total)
                total = jnp.where(label == float(b + 1), pair[:, 128:], total)
            impl_ref[f, rows, :] = total
            high, low = split(total)
            grid = dot(cf_ref[...], jnp.concatenate([high, low, high], axis=1), ((1,), (1,)))
            for h in range(2):
                piece = grid[:, h * 128 : h * 128 + 128]
                s32_ref[f, pl.ds(rt * 2 + h, 128, stride=8), :] = piece
                largest = jnp.maximum(largest, jnp.max(jnp.abs(piece).reshape(4, 32, 128), axis=1))
        return largest

    for f in range(2):
        table_copies[f].wait()
    operators(0)
    operators(1)
    largest = jnp.maximum(jnp.maximum(radial_forward(0), radial_forward(1)), 1e-30)
    inverse = QMAX / largest
    scale = largest * (1.0 / QMAX)
    for xx in range(4):
        sc_ref[0, 0, xx] = scale[xx : xx + 1]
        for rho in range(2):
            both = [
                s32_ref[f, xx * 256 : xx * 256 + 256, :].reshape(16, 2, 8, 128)[:, rho] for f in range(2)
            ]
            s16_ref[0, rho, xx] = quantize(jnp.concatenate(both, axis=1), inverse[xx : xx + 1])

    pl.semaphore_wait(barrier, 25)
    for rho in range(2):
        for k in (2, 1, 3, 0):
            x_send(0, rho, k)

    fd16_ref[...] = fd_ref[...].astype(I16)
    quarter = pl.ds(pl.multiple_of(x * 256, 256), 256)

    def state_copy(k, to, frm):
        return remote(st_ref.at[:, pl.ds(2 * to, 2)], state_ref.at[frm], us_sem.at[k], ur_sem.at[k], l_home[k])

    def quarter_copy(k, frm):
        return remote(fd16_ref.at[:, quarter], fdall_ref.at[frm, :, quarter], fs_sem.at[k], fr_sem.at[k], l_home[k])

    def depth_copy(k, frm):
        part = pl.ds(pl.multiple_of(frm * 256, 256), 256)
        return remote(fdall_ref.at[:, :, part], fdall_ref.at[:, :, part], gs_sem.at[k], gr_sem.at[k], x_home[k])

    own_state = pltpu.make_async_copy(st_ref.at[:, pl.ds(2 * zl, 2)], state_ref.at[zl], own_sem)
    own_state.start()
    fdall_ref[zl, :, quarter] = fd16_ref[:, quarter]

    z_phase(0, 0)
    for k in (2, 1, 3):
        quarter_copy(k, zl).start()
        state_copy(k, l_to[k], zl).start()
    z_phase(0, 1)

    for copy in table_copies[2:]:
        copy.wait()

    def keep_columns(rows, f, value):
        high, low = split(value)
        start, size = rows
        columns = slice(f * 128, f * 128 + 128)
        xcat_ref[pl.ds(start, size), columns] = high
        xcat_ref[pl.ds(512 + start, size), columns] = low
        xcat_ref[pl.ds(1024 + start, size), columns] = high

    def send_block(leg, rho, p, fields):
        most = jnp.maximum(jnp.abs(fields[0]), jnp.abs(fields[1]))
        most = jnp.maximum(jnp.max(most, axis=0, keepdims=True), 1e-30)
        inverse = QMAX / most
        ysc_ref[leg, rho, p] = most * (1.0 / QMAX)
        for f in range(2):
            ysend_ref[leg, rho, p, f] = quantize(fields[f], inverse)

    def theta_forward(rho):
        z_arrive(0, rho)

        def body(xx, carry):
            for zh in range(4):
                tiles = [
                    restore(zb_ref[0, rho, zh * 4 + s, xx], zsc_ref[0, 0, zh * 4 + s, xx]) for s in range(4)
                ]
                tiles = swap_groups(tiles)
                start = pl.multiple_of(xx * 128 + zh * 32, 32)
                for f in range(2):
                    rows = jnp.concatenate([tile[f * 8 : f * 8 + 8] for tile in tiles], axis=0)
                    keep_columns((start, 32), f, rows)
            return carry

        lax.fori_loop(0, 4, body, 0)
        for k in (2, 1, 3, 0):
            rows = pl.ds(pl.multiple_of(y_to[k] * 128, 128), 128)
            grid = dot(tf_ref[rows, :], xcat_ref[...])
            for h in range(2):
                send_block(0, rho, y_to[k] * 2 + h, [grid[h * 64 : h * 64 + 64, f * 128 : f * 128 + 128] for f in range(2)])
            y_send(0, rho, k)

    def axial_forward(rho):
        y_arrive(0, rho)
        for p in range(8):
            for f in range(2):
                high, low = split(restore(yrecv_ref[0, rho, p, f], yscr_ref[0, rho, p]))
                a_ref[f * 64 : f * 64 + 64, p * 128 : p * 128 + 128] = high
                a_ref[128 + f * 64 : 128 + f * 64 + 64, p * 128 : p * 128 + 128] = low
        for n in range(4):
            columns = slice(n * 256, n * 256 + 256)
            twice = dot(a_ref[...], wh_ref[:, columns])
            grid = twice[:128] + twice[128:] + dot(a_ref[:128], wl_ref[:, columns])
            keep = keep_ref[rho, :, columns]
            u0 = jnp.concatenate([state_ref[s, 0, rho, :, columns] for s in range(4)], axis=0).astype(F32)
            u1 = jnp.concatenate([state_ref[s, 1, rho, :, columns] for s in range(4)], axis=0).astype(F32)
            g0 = grid[:64]
            g1 = grid[64:]
            pull = tang_ref[rho, :, columns] * (u0 * g0 + u1 * g1)
            for f, (u, g) in enumerate(((u0, g0), (u1, g1))):
                high, low = split(pull * u - keep * g)
                f_ref[f * 64 : f * 64 + 64, columns] = high
                f_ref[128 + f * 64 : 128 + f * 64 + 64, columns] = low

    def axial_back(rho):
        for k in (2, 1, 3, 0):
            columns = pl.ds(pl.multiple_of(y_to[k] * 256, 256), 256)
            twice = dot(f_ref[...], vh_ref[:, columns])
            modes = twice[:128] + twice[128:] + dot(f_ref[:128], vl_ref[:, columns])
            for h in range(2):
                lanes = slice(h * 128, h * 128 + 128)
                send_block(1, rho, y_to[k] * 2 + h, [modes[f * 64 : f * 64 + 64, lanes] for f in range(2)])
            y_send(1, rho, k)

    def theta_back(rho):
        y_arrive(1, rho)
        for p in range(8):
            for f in range(2):
                keep_columns((p * 64, 64), f, restore(yrecv_ref[1, rho, p, f], yscr_ref[1, rho, p]))
        for k in (2, 1, 3, 0):
            xx = x_to[k]
            rows = pl.ds(pl.multiple_of(xx * 128, 128), 128)
            modes = dot(tb_ref[rows, :], xcat_ref[...])
            tiles = []
            for n in range(4):
                tiles += swap_groups([
                    jnp.concatenate(
                        [modes[n * 32 + a * 8 : n * 32 + a * 8 + 8, f * 128 : f * 128 + 128] for f in range(2)], axis=0
                    )
                    for a in range(4)
                ])
            most = jnp.abs(tiles[0])
            for tile in tiles[1:]:
                most = jnp.maximum(most, jnp.abs(tile))
            most = jnp.maximum(jnp.max(most, axis=0, keepdims=True), 1e-30)
            inverse = QMAX / most
            sc_ref[1, rho, xx] = most * (1.0 / QMAX)
            for n in range(16):
                s16_ref[1, rho, xx, n] = quantize(tiles[n], inverse)
            x_send(1, rho, k)

    theta_forward(0)

    for k in range(1, 4):
        quarter_copy(k, l_to[4 - k]).wait_recv()
    for k in range(1, 4):
        depth_copy(k, x).start()

    for k in range(1, 4):
        state_copy(k, zl, l_to[4 - k]).wait_recv()
        depth_copy(k, x_to[4 - k]).wait_recv()
    own_state.wait()
    for rho in range(2):
        for s in range(4):
            u0 = state_ref[s, 0, rho].astype(F32)
            u1 = state_ref[s, 1, rho].astype(F32)
            root = lax.rsqrt(1.0 + (u0 * u0 + u1 * u1))
            viscosity = root * lax.rsqrt(root)
            depth = fdall_ref[s].astype(jnp.int32)
            frozen = jnp.where(2 * group + rho >= R - depth, penalty, 0.0)
            keep_ref[rho, s * 16 : s * 16 + 16] = viscosity + frozen
            tang_ref[rho, s * 16 : s * 16 + 16] = 0.5 * viscosity * (root * root)

    axial_forward(0)
    axial_back(0)
    theta_forward(1)
    theta_back(0)
    axial_forward(1)
    z_phase(1, 0)
    axial_back(1)
    theta_back(1)
    z_phase(1, 1)

    for leg, rho in ((0, 0), (0, 1), (1, 0)):
        x_sent(leg, rho)
        z_sent(leg, rho)
        y_sent(leg, rho)
    x_sent(1, 1)
    y_sent(1, 1)
    for k in range(1, 4):
        state_copy(k, l_to[k], zl).wait_send()
        quarter_copy(k, zl).wait_send()
        depth_copy(k, x).wait_send()
    for rho in range(2):
        z_arrive(1, rho)
        for xx in range(4):
            tile = restore(zb_ref[1, rho, :, xx], zsc_ref[1, rho, :, xx])
            for f in range(2):
                d32_ref[f, xx * 128 : xx * 128 + 128, :] = tile[:, f * 8 : f * 8 + 8].reshape(128, 128)
        for f in range(2):
            for tg in range(8):
                high, low = split(d32_ref[f, pl.ds(tg, 64, stride=8), :])
                gamma = dot(jnp.concatenate([high, low, high], axis=0), cb_ref[rho], ((0,), (0,)))
                rows = slice(tg * 128, tg * 128 + 128)
                before = impl_ref if rho == 0 else out_ref
                out_ref[f, rows, :] = before[f, rows, :] + step_dt * gamma
    z_sent(1, 1)


def on_device(adj_coef, grid_state, block_index, frozen_depth, inv_blocks):
    constants = [jnp.asarray(table) for table in tables()]
    vmem = pl.BlockSpec(memory_space=pltpu.VMEM)
    hbm = pl.BlockSpec(memory_space=pltpu.HBM)
    dma = pltpu.SemaphoreType.DMA
    scratch = [
        pltpu.VMEM((2, 1024, 128), F32),
        pltpu.VMEM((NB, 2, 128, 128), F32),
        pltpu.VMEM((512, 1536), BF16),
        pltpu.VMEM((512, 1536), BF16),
        pltpu.VMEM((NZ, NZ), BF16),
        pltpu.VMEM((NZ, NZ), BF16),
        pltpu.VMEM((NZ, NZ), BF16),
        pltpu.VMEM((NZ, NZ), BF16),
        pltpu.VMEM((2, NB // 2, 384, 256), BF16),
        pltpu.VMEM((2, 1024, 128), F32),
        pltpu.VMEM((2, 1024, 128), F32),
        pltpu.VMEM((2, 512, 128), F32),
        pltpu.VMEM((2, 2, 4, 16, 16, 128), I16),
        pltpu.VMEM((2, 2, 4, 16, 16, 128), I16),
        pltpu.VMEM((2, 2, 16, 4, 16, 128), I16),
        pltpu.VMEM((2, 2, 4, 1, 128), F32),
        pltpu.VMEM((2, 2, 4, 1, 128), F32),
        pltpu.VMEM((2, 2, 16, 4, 1, 128), F32),
        pltpu.VMEM((2, 2, 8, 2, 64, 128), I16),
        pltpu.VMEM((2, 2, 8, 2, 64, 128), I16),
        pltpu.VMEM((2, 2, 8, 1, 128), F32),
        pltpu.VMEM((2, 2, 8, 1, 128), F32),
        pltpu.VMEM((4, 2, 2, 16, NZ), BF16),
        pltpu.VMEM((16, NZ), I16),
        pltpu.VMEM((4, 16, NZ), I16),
        pltpu.VMEM((2, 64, NZ), F32),
        pltpu.VMEM((2, 64, NZ), F32),
        pltpu.VMEM((1536, 256), BF16),
        pltpu.VMEM((256, NZ), BF16),
        pltpu.VMEM((256, NZ), BF16),
        dma((8,)),
        dma((2, 2, 4)), dma((2, 2, 4)), dma((2, 2, 16)), dma((2, 2, 16)), dma((2, 2, 8)), dma((2, 2, 8)),
        dma((2, 2, 4)), dma((2, 2, 4)), dma((2, 2, 16)), dma((2, 2, 16)), dma((2, 2, 8)), dma((2, 2, 8)),
        dma((4,)), dma((4,)), dma((4,)), dma((4,)), dma((4,)), dma((4,)), dma,
    ]
    step = pl.pallas_call(
        kernel,
        out_shape=jax.ShapeDtypeStruct((2, 1024, R), F32),
        in_specs=[hbm, hbm, vmem, vmem, hbm, vmem, vmem] + [hbm] * 6,
        out_specs=vmem,
        scratch_shapes=scratch,
        compiler_params=pltpu.CompilerParams(
            collective_id=0, has_side_effects=True, vmem_limit_bytes=56 * 1024 * 1024
        ),
    )
    flat = adj_coef.reshape(2, 1024, R)
    result = step(flat, grid_state, block_index, frozen_depth, inv_blocks, *constants)
    return result.reshape(2, 32, 32, R)


def solution(mesh):
    placed = (
        P(None, "az", "ax", None),
        P(None, "az", "ax", None),
        P("az", "ax"),
        P("ax", None),
        P(),
    )
    return jax.shard_map(
        on_device, mesh=mesh, in_specs=placed, out_specs=P(None, "az", "ax", None), check_vma=False
    )
```

```python
import math

import jax
import jax.numpy as jnp
import ml_dtypes
import numpy as np
from jax import lax
from jax.experimental import pallas as pl
from jax.experimental.pallas import tpu as pltpu
from jax.sharding import PartitionSpec as P

NT = 512
NZ = 1024
R = 128
NB = 8
penalty = 2.0
step_dt = 0.3
QMAX = 32767.0
ROUNDER = 12582912.0
F32 = jnp.float32
BF16 = jnp.bfloat16
I16 = jnp.int16
MESH = pl.DeviceIdType.MESH


def hartley(count):
    index = np.arange(count, dtype=np.int64)
    angle = (index[:, None] * index[None, :] % count) * (2.0 * math.pi / count)
    return (np.cos(angle) + np.sin(angle)) / math.sqrt(count)


def chebyshev(count):
    index = np.arange(count, dtype=np.int64)
    angle = (index[:, None] * index[None, :] % (2 * (count - 1))) * (math.pi / (count - 1))
    return np.cos(angle) * math.sqrt(2.0 / count)


def parts(table):
    high = table.astype(ml_dtypes.bfloat16)
    low = (table - high.astype(np.float64)).astype(ml_dtypes.bfloat16)
    return high, low


def tables():
    q, zl, i = np.meshgrid(np.arange(8), np.arange(4), np.arange(16), indexing="ij")
    theta_order = (16 * (zl * 8 + q) + i).reshape(-1)
    az, t4, tg = np.meshgrid(np.arange(16), np.arange(4), np.arange(8), indexing="ij")
    mode_order = (32 * az + tg * 4 + t4).reshape(-1)
    q, zl, i = np.meshgrid(np.arange(8), np.arange(4), np.arange(32), indexing="ij")
    axial_order = (32 * (zl * 8 + q) + i).reshape(-1)
    theta = hartley(NT)[theta_order][:, mode_order]
    axial = hartley(NZ)[axial_order]
    radial = chebyshev(R)
    ch, cl = parts(radial)
    dh, dl = parts(np.stack([radial[0::2], radial[1::2]]))
    th, tl = parts(theta)
    bh, bl = parts(theta.T)
    wh, wl = parts(axial)
    vh, vl = parts(axial.T)
    return [
        np.concatenate([ch, ch, cl], axis=1),
        np.stack([np.concatenate([dh[i], dh[i], dl[i]], axis=0) for i in range(2)]),
        np.concatenate([th, th, tl], axis=1),
        np.concatenate([bh, bh, bl], axis=1),
        wh,
        wl,
        np.ascontiguousarray(vh),
        np.ascontiguousarray(vl),
    ]


def split(value):
    high = value.astype(BF16)
    low = (value - high.astype(F32)).astype(BF16)
    return high, low


def dot(a, b, dims=((1,), (0,))):
    return lax.dot_general(a, b, (dims, ((), ())), preferred_element_type=F32)


def swap_groups(tiles):
    lane = lax.broadcasted_iota(jnp.int32, tiles[0].shape, 1)
    first = lane < 64
    even = lane % 64 < 32
    t0, t1, t2, t3 = tiles
    a0 = jnp.where(first, t0, pltpu.roll(t2, 64, 1))
    a2 = jnp.where(first, pltpu.roll(t0, 64, 1), t2)
    a1 = jnp.where(first, t1, pltpu.roll(t3, 64, 1))
    a3 = jnp.where(first, pltpu.roll(t1, 64, 1), t3)
    b0 = jnp.where(even, a0, pltpu.roll(a1, 32, 1))
    b1 = jnp.where(even, pltpu.roll(a0, 96, 1), a1)
    b2 = jnp.where(even, a2, pltpu.roll(a3, 32, 1))
    b3 = jnp.where(even, pltpu.roll(a2, 96, 1), a3)
    return [b0, b1, b2, b3]


def quantize(value, inverse):
    whole = (value * inverse + ROUNDER) - ROUNDER
    return whole.astype(jnp.int32).astype(I16)


def restore(value, scale):
    return value.astype(jnp.int32).astype(F32) * scale


def kernel(
    x_in, st_ref, bi_ref, fd_ref, inv_in, cf_ref, cb_ref,
    tf_in, tb_in, wh_in, wl_in, vh_in, vl_in,
    out_ref,
    x_ref, inv_ref, tf_ref, tb_ref, wh_ref, wl_ref, vh_ref, vl_ref,
    wc_ref, impl_ref, s32_ref, d32_ref,
    s16_ref, xb_ref, zb_ref, sc_ref, xsc_ref, zsc_ref,
    ysend_ref, yrecv_ref, ysc_ref, yscr_ref,
    state_ref, fd16_ref, fdall_ref, keep_ref, tang_ref,
    xcat_ref, a_ref, f_ref,
    table_sem, xs_sem, xr_sem, zs_sem, zr_sem, ys_sem, yr_sem,
    xcs_sem, xcr_sem, zcs_sem, zcr_sem, ycs_sem, ycr_sem,
    us_sem, ur_sem, fs_sem, fr_sem, gs_sem, gr_sem, own_sem,
):
    az = lax.axis_index("az")
    ax = lax.axis_index("ax")
    x = lax.div(az, 4)
    zl = lax.div(ax, 8)
    q = lax.rem(ax, 8)
    y = lax.div(q, 2)
    core = lax.rem(q, 2)
    z = lax.rem(az, 4) * 4 + zl
    group = x * 16 + z

    x_to = [lax.rem(x + k, 4) for k in range(4)]
    z_to = [lax.rem(z + k, 16) for k in range(16)]
    x_home = [(xx * 4 + lax.rem(az, 4), ax) for xx in x_to]
    z_home = [(x * 4 + lax.div(zz, 4), lax.rem(zz, 4) * 8 + q) for zz in z_to]
    y_to = [lax.rem(y + k, 4) for k in range(4)]
    l_to = [lax.rem(zl + k, 4) for k in range(4)]
    l_home = [(az, ll * 8 + q) for ll in l_to]

    def y_home(k, h):
        return (az, zl * 8 + y_to[k] * 2 + h)

    def remote(src, dst, send, recv, device):
        return pltpu.make_async_remote_copy(
            src_ref=src, dst_ref=dst, send_sem=send, recv_sem=recv, device_id=device, device_id_type=MESH
        )

    table_copies = [
        pltpu.make_async_copy(src, dst, table_sem.at[n])
        for n, (src, dst) in enumerate(
            [
                (inv_in, inv_ref), (x_in, x_ref), (tf_in, tf_ref), (tb_in, tb_ref),
                (wh_in, wh_ref), (wl_in, wl_ref), (vh_in, vh_ref), (vl_in, vl_ref),
            ]
        )
    ]
    for copy in table_copies:
        copy.start()
    barrier = pltpu.get_barrier_semaphore()
    homes = x_home[1:] + z_home[1:] + [y_home(k, h) for k in range(1, 4) for h in range(2)] + [y_home(0, 1 - core)]
    for home in homes:
        pl.semaphore_signal(barrier, inc=1, device_id=home, device_id_type=MESH)

    def x_copies(leg, rho, k, to, frm, home):
        data = [
            remote(s16_ref.at[leg, rho, to], xb_ref.at[leg, rho, :, frm], xs_sem.at[leg, rho, k], xr_sem.at[leg, rho, k], home),
        ]
        if leg == 0 and rho == 1:
            return data
        return data + [
            remote(sc_ref.at[leg, rho, to], xsc_ref.at[leg, rho, frm], xcs_sem.at[leg, rho, k], xcr_sem.at[leg, rho, k], home),
        ]

    def z_copies(leg, rho, k, to, frm, home):
        data = [
            remote(xb_ref.at[leg, rho, to], zb_ref.at[leg, rho, frm], zs_sem.at[leg, rho, k], zr_sem.at[leg, rho, k], home),
        ]
        if leg == 0 and rho == 1:
            return data
        return data + [
            remote(xsc_ref.at[leg, rho], zsc_ref.at[leg, rho, frm], zcs_sem.at[leg, rho, k], zcr_sem.at[leg, rho, k], home),
        ]

    def exchange(copies, place, homes, count):
        def start(leg, rho):
            order = sorted(range(1, count), key=lambda k: (-min(k, count - k), k))
            for k in order:
                for copy in copies(leg, rho, k, place[k], place[0], homes[k]):
                    copy.start()

        def arrive(leg, rho):
            for k in range(1, count):
                for copy in copies(leg, rho, k, place[0], place[count - k], homes[k]):
                    copy.wait_recv()

        def sent(leg, rho):
            for k in range(1, count):
                for copy in copies(leg, rho, k, place[k], place[0], homes[k]):
                    copy.wait_send()

        return start, arrive, sent

    _, x_arrive, x_sent = exchange(x_copies, x_to, x_home, 4)
    z_start, z_arrive, z_sent = exchange(z_copies, z_to, z_home, 16)

    def y_copies(leg, rho, k, h, frm, frm_core):
        to = y_to[k] * 2 + h
        send = 2 * k + h
        recv = 2 * k + frm_core
        return [
            remote(ysend_ref.at[leg, rho, to], yrecv_ref.at[leg, rho, frm], ys_sem.at[leg, rho, send], yr_sem.at[leg, rho, recv], y_home(k, h)),
            remote(ysc_ref.at[leg, rho, to], yscr_ref.at[leg, rho, frm], ycs_sem.at[leg, rho, send], ycr_sem.at[leg, rho, recv], y_home(k, h)),
        ]

    def y_partners(k):
        return (0, 1) if k else (1 - core,)

    def y_send(leg, rho, k):
        for h in y_partners(k):
            for copy in y_copies(leg, rho, k, h, q, core):
                copy.start()
        if k == 0:
            yrecv_ref[leg, rho, q] = ysend_ref[leg, rho, q]
            yscr_ref[leg, rho, q] = ysc_ref[leg, rho, q]

    def y_arrive(leg, rho):
        for k in (2, 1, 3, 0):
            for h in y_partners(k):
                for copy in y_copies(leg, rho, k, core, y_to[(4 - k) % 4] * 2 + h, h):
                    copy.wait_recv()

    def y_sent(leg, rho):
        for k in range(4):
            for h in y_partners(k):
                for copy in y_copies(leg, rho, k, h, q, core):
                    copy.wait_send()

    def x_send(leg, rho, k):
        if k:
            for copy in x_copies(leg, rho, k, x_to[k], x, x_home[k]):
                copy.start()
        else:
            xb_ref[leg, rho, :, x] = s16_ref[leg, rho, x]
            if leg == 1 or rho == 0:
                xsc_ref[leg, rho, x] = sc_ref[leg, rho, x]

    def z_phase(leg, rho):
        x_arrive(leg, rho)
        z_start(leg, rho)
        zb_ref[leg, rho, z] = xb_ref[leg, rho, z]
        if leg == 1 or rho == 0:
            zsc_ref[leg, rho, z] = xsc_ref[leg, rho]

    def operators(f):
        for b in range(NB):
            high, low = split(inv_ref[b, f].T)
            columns = slice(b % 2 * 128, b % 2 * 128 + 128)
            wc_ref[f, b // 2, 0:128, columns] = high
            wc_ref[f, b // 2, 128:256, columns] = high
            wc_ref[f, b // 2, 256:384, columns] = low

    def radial_forward(f):
        eye = lax.broadcasted_iota(jnp.int32, (32, 32), 0) == lax.broadcasted_iota(jnp.int32, (32, 32), 1)
        ones = jnp.ones((32, 128), BF16)
        largest = jnp.zeros((4, 128), F32)
        for rt in range(4):
            rows = slice(rt * 256, rt * 256 + 256)
            labels = bi_ref[rt * 8 : rt * 8 + 8, :].astype(F32)
            spread = [jnp.where(eye, jnp.broadcast_to(labels[t : t + 1], (32, 32)), 0.0) for t in range(8)]
            label = dot(jnp.concatenate(spread, axis=0).astype(BF16), ones)
            high, low = split(x_ref[f, rows, :])
            both = jnp.concatenate([high, low, high], axis=1)
            total = jnp.zeros((256, 128), F32)
            for b in range(0, NB, 2):
                pair = dot(both, wc_ref[f, b // 2])
                total = jnp.where(label == float(b), pair[:, :128], total)
                total = jnp.where(label == float(b + 1), pair[:, 128:], total)
            impl_ref[f, rows, :] = total
            high, low = split(total)
            grid = dot(cf_ref[...], jnp.concatenate([high, low, high], axis=1), ((1,), (1,)))
            for h in range(2):
                piece = grid[:, h * 128 : h * 128 + 128]
                s32_ref[f, pl.ds(rt * 2 + h, 128, stride=8), :] = piece
                largest = jnp.maximum(largest, jnp.max(jnp.abs(piece).reshape(4, 32, 128), axis=1))
        return largest

    for f in range(2):
        table_copies[f].wait()
    operators(0)
    operators(1)
    largest = radial_forward(0)

    pl.semaphore_wait(barrier, 25)

    fd16_ref[...] = fd_ref[...].astype(I16)
    quarter = pl.ds(pl.multiple_of(x * 256, 256), 256)

    def state_copy(k, to, frm):
        return remote(st_ref.at[:, pl.ds(2 * to, 2)], state_ref.at[frm], us_sem.at[k], ur_sem.at[k], l_home[k])

    def quarter_copy(k, frm):
        return remote(fd16_ref.at[:, quarter], fdall_ref.at[frm, :, quarter], fs_sem.at[k], fr_sem.at[k], l_home[k])

    def depth_copy(k, frm):
        part = pl.ds(pl.multiple_of(frm * 256, 256), 256)
        return remote(fdall_ref.at[:, :, part], fdall_ref.at[:, :, part], gs_sem.at[k], gr_sem.at[k], x_home[k])

    own_state = pltpu.make_async_copy(st_ref.at[:, pl.ds(2 * zl, 2)], state_ref.at[zl], own_sem)
    own_state.start()
    fdall_ref[zl, :, quarter] = fd16_ref[:, quarter]
    for k in (2, 1, 3):
        quarter_copy(k, zl).start()
        state_copy(k, l_to[k], zl).start()

    largest = jnp.maximum(jnp.maximum(largest, radial_forward(1)), 1e-30)
    inverse = QMAX / largest
    scale = largest * (1.0 / QMAX)
    for xx in range(4):
        sc_ref[0, 0, xx] = scale[xx : xx + 1]
        for rho in range(2):
            both = [
                s32_ref[f, xx * 256 : xx * 256 + 256, :].reshape(16, 2, 8, 128)[:, rho] for f in range(2)
            ]
            s16_ref[0, rho, xx] = quantize(jnp.concatenate(both, axis=1), inverse[xx : xx + 1])

    for rho in range(2):
        for k in (2, 1, 3, 0):
            x_send(0, rho, k)
    z_phase(0, 0)
    z_phase(0, 1)

    for copy in table_copies[2:]:
        copy.wait()

    def keep_columns(rows, f, value):
        high, low = split(value)
        start, size = rows
        columns = slice(f * 128, f * 128 + 128)
        xcat_ref[pl.ds(start, size), columns] = high
        xcat_ref[pl.ds(512 + start, size), columns] = low
        xcat_ref[pl.ds(1024 + start, size), columns] = high

    def send_block(leg, rho, p, fields):
        most = jnp.maximum(jnp.abs(fields[0]), jnp.abs(fields[1]))
        most = jnp.maximum(jnp.max(most, axis=0, keepdims=True), 1e-30)
        inverse = QMAX / most
        ysc_ref[leg, rho, p] = most * (1.0 / QMAX)
        for f in range(2):
            ysend_ref[leg, rho, p, f] = quantize(fields[f], inverse)

    def theta_forward(rho):
        z_arrive(0, rho)

        def body(xx, carry):
            for zh in range(4):
                tiles = [
                    restore(zb_ref[0, rho, zh * 4 + s, xx], zsc_ref[0, 0, zh * 4 + s, xx]) for s in range(4)
                ]
                tiles = swap_groups(tiles)
                start = pl.multiple_of(xx * 128 + zh * 32, 32)
                for f in range(2):
                    rows = jnp.concatenate([tile[f * 8 : f * 8 + 8] for tile in tiles], axis=0)
                    keep_columns((start, 32), f, rows)
            return carry

        lax.fori_loop(0, 4, body, 0)
        for k in (2, 1, 3, 0):
            rows = pl.ds(pl.multiple_of(y_to[k] * 128, 128), 128)
            grid = dot(tf_ref[rows, :], xcat_ref[...])
            for h in range(2):
                send_block(0, rho, y_to[k] * 2 + h, [grid[h * 64 : h * 64 + 64, f * 128 : f * 128 + 128] for f in range(2)])
            y_send(0, rho, k)

    def axial_forward(rho):
        y_arrive(0, rho)
        for p in range(8):
            for f in range(2):
                high, low = split(restore(yrecv_ref[0, rho, p, f], yscr_ref[0, rho, p]))
                a_ref[f * 64 : f * 64 + 64, p * 128 : p * 128 + 128] = high
                a_ref[128 + f * 64 : 128 + f * 64 + 64, p * 128 : p * 128 + 128] = low
        for n in range(4):
            columns = slice(n * 256, n * 256 + 256)
            twice = dot(a_ref[...], wh_ref[:, columns])
            grid = twice[:128] + twice[128:] + dot(a_ref[:128], wl_ref[:, columns])
            keep = keep_ref[rho, :, columns]
            u0 = jnp.concatenate([state_ref[s, 0, rho, :, columns] for s in range(4)], axis=0).astype(F32)
            u1 = jnp.concatenate([state_ref[s, 1, rho, :, columns] for s in range(4)], axis=0).astype(F32)
            g0 = grid[:64]
            g1 = grid[64:]
            pull = tang_ref[rho, :, columns] * (u0 * g0 + u1 * g1)
            for f, (u, g) in enumerate(((u0, g0), (u1, g1))):
                high, low = split(pull * u - keep * g)
                f_ref[f * 64 : f * 64 + 64, columns] = high
                f_ref[128 + f * 64 : 128 + f * 64 + 64, columns] = low

    def axial_back(rho):
        for k in (2, 1, 3, 0):
            columns = pl.ds(pl.multiple_of(y_to[k] * 256, 256), 256)
            twice = dot(f_ref[...], vh_ref[:, columns])
            modes = twice[:128] + twice[128:] + dot(f_ref[:128], vl_ref[:, columns])
            for h in range(2):
                lanes = slice(h * 128, h * 128 + 128)
                send_block(1, rho, y_to[k] * 2 + h, [modes[f * 64 : f * 64 + 64, lanes] for f in range(2)])
            y_send(1, rho, k)

    def theta_back(rho):
        y_arrive(1, rho)
        for p in range(8):
            for f in range(2):
                keep_columns((p * 64, 64), f, restore(yrecv_ref[1, rho, p, f], yscr_ref[1, rho, p]))
        for k in (2, 1, 3, 0):
            xx = x_to[k]
            rows = pl.ds(pl.multiple_of(xx * 128, 128), 128)
            modes = dot(tb_ref[rows, :], xcat_ref[...])
            tiles = []
            for n in range(4):
                tiles += swap_groups([
                    jnp.concatenate(
                        [modes[n * 32 + a * 8 : n * 32 + a * 8 + 8, f * 128 : f * 128 + 128] for f in range(2)], axis=0
                    )
                    for a in range(4)
                ])
            most = jnp.abs(tiles[0])
            for tile in tiles[1:]:
                most = jnp.maximum(most, jnp.abs(tile))
            most = jnp.maximum(jnp.max(most, axis=0, keepdims=True), 1e-30)
            inverse = QMAX / most
            sc_ref[1, rho, xx] = most * (1.0 / QMAX)
            for n in range(16):
                s16_ref[1, rho, xx, n] = quantize(tiles[n], inverse)
            x_send(1, rho, k)

    theta_forward(0)

    for k in range(1, 4):
        quarter_copy(k, l_to[4 - k]).wait_recv()
    for k in range(1, 4):
        depth_copy(k, x).start()

    for k in range(1, 4):
        state_copy(k, zl, l_to[4 - k]).wait_recv()
        depth_copy(k, x_to[4 - k]).wait_recv()
    own_state.wait()
    for rho in range(2):
        for s in range(4):
            u0 = state_ref[s, 0, rho].astype(F32)
            u1 = state_ref[s, 1, rho].astype(F32)
            root = lax.rsqrt(1.0 + (u0 * u0 + u1 * u1))
            viscosity = root * lax.rsqrt(root)
            depth = fdall_ref[s].astype(jnp.int32)
            frozen = jnp.where(2 * group + rho >= R - depth, penalty, 0.0)
            keep_ref[rho, s * 16 : s * 16 + 16] = viscosity + frozen
            tang_ref[rho, s * 16 : s * 16 + 16] = 0.5 * viscosity * (root * root)

    axial_forward(0)
    axial_back(0)
    theta_forward(1)
    theta_back(0)
    axial_forward(1)
    z_phase(1, 0)
    axial_back(1)
    theta_back(1)
    z_phase(1, 1)

    for leg, rho in ((0, 0), (0, 1), (1, 0)):
        x_sent(leg, rho)
        z_sent(leg, rho)
        y_sent(leg, rho)
    x_sent(1, 1)
    y_sent(1, 1)
    for k in range(1, 4):
        state_copy(k, l_to[k], zl).wait_send()
        quarter_copy(k, zl).wait_send()
        depth_copy(k, x).wait_send()
    for rho in range(2):
        z_arrive(1, rho)
        for xx in range(4):
            tile = restore(zb_ref[1, rho, :, xx], zsc_ref[1, rho, :, xx])
            for f in range(2):
                d32_ref[f, xx * 128 : xx * 128 + 128, :] = tile[:, f * 8 : f * 8 + 8].reshape(128, 128)
        for f in range(2):
            for tg in range(8):
                high, low = split(d32_ref[f, pl.ds(tg, 64, stride=8), :])
                gamma = dot(jnp.concatenate([high, low, high], axis=0), cb_ref[rho], ((0,), (0,)))
                rows = slice(tg * 128, tg * 128 + 128)
                before = impl_ref if rho == 0 else out_ref
                out_ref[f, rows, :] = before[f, rows, :] + step_dt * gamma
    z_sent(1, 1)


def on_device(adj_coef, grid_state, block_index, frozen_depth, inv_blocks):
    constants = [jnp.asarray(table) for table in tables()]
    vmem = pl.BlockSpec(memory_space=pltpu.VMEM)
    hbm = pl.BlockSpec(memory_space=pltpu.HBM)
    dma = pltpu.SemaphoreType.DMA
    scratch = [
        pltpu.VMEM((2, 1024, 128), F32),
        pltpu.VMEM((NB, 2, 128, 128), F32),
        pltpu.VMEM((512, 1536), BF16),
        pltpu.VMEM((512, 1536), BF16),
        pltpu.VMEM((NZ, NZ), BF16),
        pltpu.VMEM((NZ, NZ), BF16),
        pltpu.VMEM((NZ, NZ), BF16),
        pltpu.VMEM((NZ, NZ), BF16),
        pltpu.VMEM((2, NB // 2, 384, 256), BF16),
        pltpu.VMEM((2, 1024, 128), F32),
        pltpu.VMEM((2, 1024, 128), F32),
        pltpu.VMEM((2, 512, 128), F32),
        pltpu.VMEM((2, 2, 4, 16, 16, 128), I16),
        pltpu.VMEM((2, 2, 16, 4, 16, 128), I16),
        pltpu.VMEM((2, 2, 16, 4, 16, 128), I16),
        pltpu.VMEM((2, 2, 4, 1, 128), F32),
        pltpu.VMEM((2, 2, 4, 1, 128), F32),
        pltpu.VMEM((2, 2, 16, 4, 1, 128), F32),
        pltpu.VMEM((2, 2, 8, 2, 64, 128), I16),
        pltpu.VMEM((2, 2, 8, 2, 64, 128), I16),
        pltpu.VMEM((2, 2, 8, 1, 128), F32),
        pltpu.VMEM((2, 2, 8, 1, 128), F32),
        pltpu.VMEM((4, 2, 2, 16, NZ), BF16),
        pltpu.VMEM((16, NZ), I16),
        pltpu.VMEM((4, 16, NZ), I16),
        pltpu.VMEM((2, 64, NZ), F32),
        pltpu.VMEM((2, 64, NZ), F32),
        pltpu.VMEM((1536, 256), BF16),
        pltpu.VMEM((256, NZ), BF16),
        pltpu.VMEM((256, NZ), BF16),
        dma((8,)),
        dma((2, 2, 4)), dma((2, 2, 4)), dma((2, 2, 16)), dma((2, 2, 16)), dma((2, 2, 8)), dma((2, 2, 8)),
        dma((2, 2, 4)), dma((2, 2, 4)), dma((2, 2, 16)), dma((2, 2, 16)), dma((2, 2, 8)), dma((2, 2, 8)),
        dma((4,)), dma((4,)), dma((4,)), dma((4,)), dma((4,)), dma((4,)), dma,
    ]
    step = pl.pallas_call(
        kernel,
        out_shape=jax.ShapeDtypeStruct((2, 1024, R), F32),
        in_specs=[hbm, hbm, vmem, vmem, hbm, vmem, vmem] + [hbm] * 6,
        out_specs=vmem,
        scratch_shapes=scratch,
        compiler_params=pltpu.CompilerParams(
            collective_id=0, has_side_effects=True, vmem_limit_bytes=56 * 1024 * 1024
        ),
    )
    flat = adj_coef.reshape(2, 1024, R)
    result = step(flat, grid_state, block_index, frozen_depth, inv_blocks, *constants)
    return result.reshape(2, 32, 32, R)


def solution(mesh):
    placed = (
        P(None, "az", "ax", None),
        P(None, "az", "ax", None),
        P("az", "ax"),
        P("ax", None),
        P(),
    )
    return jax.shard_map(
        on_device, mesh=mesh, in_specs=placed, out_specs=P(None, "az", "ax", None), check_vma=False
    )
```

```python
import math

import jax
import jax.numpy as jnp
import ml_dtypes
import numpy as np
from jax import lax
from jax.experimental import pallas as pl
from jax.experimental.pallas import tpu as pltpu
from jax.sharding import PartitionSpec as P

NT = 512
NZ = 1024
R = 128
NB = 8
penalty = 2.0
step_dt = 0.3
QMAX = 32767.0
ROUNDER = 12582912.0
F32 = jnp.float32
BF16 = jnp.bfloat16
I16 = jnp.int16
MESH = pl.DeviceIdType.MESH


def hartley(count):
    index = np.arange(count, dtype=np.int64)
    angle = (index[:, None] * index[None, :] % count) * (2.0 * math.pi / count)
    return (np.cos(angle) + np.sin(angle)) / math.sqrt(count)


def chebyshev(count):
    index = np.arange(count, dtype=np.int64)
    angle = (index[:, None] * index[None, :] % (2 * (count - 1))) * (math.pi / (count - 1))
    return np.cos(angle) * math.sqrt(2.0 / count)


def parts(table):
    high = table.astype(ml_dtypes.bfloat16)
    low = (table - high.astype(np.float64)).astype(ml_dtypes.bfloat16)
    return high, low


def tables():
    q, zl, i = np.meshgrid(np.arange(8), np.arange(2), np.arange(16), indexing="ij")
    theta_order = (16 * (zl * 8 + q) + i).reshape(-1)
    az, half, tg = np.meshgrid(np.arange(16), np.arange(2), np.arange(8), indexing="ij")
    mode_order = (32 * az + tg * 4 + 2 * half).reshape(-1)
    pair, lane = np.meshgrid(np.arange(4), np.arange(128), indexing="ij")
    device = 2 * pair + lane % 2
    axial_order = (32 * (lane // 32 * 8 + device) + lane % 32 // 2 * 2).reshape(-1)
    theta_full = hartley(NT)[theta_order]
    theta = np.stack([theta_full[:, mode_order + par] for par in range(2)])
    axial = np.stack([hartley(NZ)[axial_order + par][:, : NZ // 2] for par in range(2)])
    radial = chebyshev(R)
    ch, cl = parts(radial)
    dh, dl = parts(np.stack([radial[0::2], radial[1::2]]))
    th, tl = parts(theta)
    bh, bl = parts(theta.transpose(0, 2, 1))
    wh, wl = parts(axial)
    vh, vl = parts(np.ascontiguousarray(axial.transpose(0, 2, 1)))
    return [
        np.concatenate([ch, ch, cl], axis=1),
        np.stack([np.concatenate([dh[i], dh[i], dl[i]], axis=0) for i in range(2)]),
        np.concatenate([th, th, tl], axis=2),
        np.concatenate([bh, bh, bl], axis=2),
        wh,
        wl,
        vh,
        vl,
    ]


def split(value):
    high = value.astype(BF16)
    low = (value - high.astype(F32)).astype(BF16)
    return high, low


def dot(a, b, dims=((1,), (0,))):
    return lax.dot_general(a, b, (dims, ((), ())), preferred_element_type=F32)


def swap_groups(tiles):
    lane = lax.broadcasted_iota(jnp.int32, tiles[0].shape, 1)
    first = lane < 64
    even = lane % 64 < 32
    t0, t1, t2, t3 = tiles
    a0 = jnp.where(first, t0, pltpu.roll(t2, 64, 1))
    a2 = jnp.where(first, pltpu.roll(t0, 64, 1), t2)
    a1 = jnp.where(first, t1, pltpu.roll(t3, 64, 1))
    a3 = jnp.where(first, pltpu.roll(t1, 64, 1), t3)
    b0 = jnp.where(even, a0, pltpu.roll(a1, 32, 1))
    b1 = jnp.where(even, pltpu.roll(a0, 96, 1), a1)
    b2 = jnp.where(even, a2, pltpu.roll(a3, 32, 1))
    b3 = jnp.where(even, pltpu.roll(a2, 96, 1), a3)
    return [b0, b1, b2, b3]


def swap_parity(first, second):
    even = lax.broadcasted_iota(jnp.int32, first.shape, 1) % 2 == 0
    return (
        jnp.where(even, first, pltpu.roll(second, 1, 1)),
        jnp.where(even, pltpu.roll(first, 127, 1), second),
    )


def quantize(value, inverse):
    whole = (value * inverse + ROUNDER) - ROUNDER
    return whole.astype(jnp.int32).astype(I16)


def restore(value, scale):
    return value.astype(jnp.int32).astype(F32) * scale


def kernel(
    x_in, st_ref, bi_ref, fd_ref, inv_in, cf_ref, cb_ref,
    tf_in, tb_in, wh_in, wl_in, vh_in, vl_in,
    out_ref,
    x_ref, inv_ref, tf_ref, tb_ref, wh_ref, wl_ref, vh_ref, vl_ref,
    wc_ref, impl_ref, s32_ref, d32_ref,
    s16_ref, xb_ref, zb_ref, sc_ref, xsc_ref, zsc_ref,
    ysend_ref, yrecv_ref, ysc_ref, yscr_ref,
    state_ref, fd16_ref, fdall_ref, keep_ref, tang_ref,
    xcat_ref, a_ref, f_ref, t32_ref,
    table_sem, xs_sem, xr_sem, zs_sem, zr_sem, ys_sem, yr_sem,
    xcs_sem, xcr_sem, zcs_sem, zcr_sem, ycs_sem, ycr_sem,
    us_sem, ur_sem, fs_sem, fr_sem, gs_sem, gr_sem, own_sem,
):
    az = lax.axis_index("az")
    ax = lax.axis_index("ax")
    x = lax.div(az, 4)
    zl = lax.div(ax, 8)
    q = lax.rem(ax, 8)
    y = lax.div(q, 2)
    core = lax.rem(q, 2)
    z = lax.rem(az, 4) * 4 + zl
    group = x * 16 + z

    x_to = [lax.rem(x + k, 4) for k in range(4)]
    z_to = [lax.rem(z + k, 16) for k in range(16)]
    x_home = [(xx * 4 + lax.rem(az, 4), ax) for xx in x_to]
    z_home = [(x * 4 + lax.div(zz, 4), lax.rem(zz, 4) * 8 + q) for zz in z_to]
    y_to = [lax.rem(y + k, 4) for k in range(4)]
    l_to = [lax.rem(zl + k, 4) for k in range(4)]
    l_home = [(az, ll * 8 + q) for ll in l_to]

    def y_home(k, h):
        return (az, zl * 8 + y_to[k] * 2 + h)

    def remote(src, dst, send, recv, device):
        return pltpu.make_async_remote_copy(
            src_ref=src, dst_ref=dst, send_sem=send, recv_sem=recv, device_id=device, device_id_type=MESH
        )

    table_copies = [
        pltpu.make_async_copy(src, dst, table_sem.at[n])
        for n, (src, dst) in enumerate(
            [
                (inv_in, inv_ref), (x_in, x_ref), (tf_in, tf_ref), (tb_in, tb_ref),
                (wh_in, wh_ref), (wl_in, wl_ref), (vh_in, vh_ref), (vl_in, vl_ref),
            ]
        )
    ]
    for copy in table_copies:
        copy.start()
    barrier = pltpu.get_barrier_semaphore()
    homes = x_home[1:] + z_home[1:] + [y_home(k, h) for k in range(1, 4) for h in range(2)] + [y_home(0, 1 - core)]
    for home in homes:
        pl.semaphore_signal(barrier, inc=1, device_id=home, device_id_type=MESH)

    def x_copies(leg, rho, k, to, frm, home):
        data = [
            remote(s16_ref.at[leg, rho, to], xb_ref.at[leg, rho, :, frm], xs_sem.at[leg, rho, k], xr_sem.at[leg, rho, k], home),
        ]
        if leg == 0 and rho == 1:
            return data
        return data + [
            remote(sc_ref.at[leg, rho, to], xsc_ref.at[leg, rho, frm], xcs_sem.at[leg, rho, k], xcr_sem.at[leg, rho, k], home),
        ]

    def z_copies(leg, rho, k, to, frm, home):
        data = [
            remote(xb_ref.at[leg, rho, to], zb_ref.at[leg, rho, frm], zs_sem.at[leg, rho, k], zr_sem.at[leg, rho, k], home),
        ]
        if leg == 0 and rho == 1:
            return data
        return data + [
            remote(xsc_ref.at[leg, rho], zsc_ref.at[leg, rho, frm], zcs_sem.at[leg, rho, k], zcr_sem.at[leg, rho, k], home),
        ]

    def exchange(copies, place, homes, count):
        def start(leg, rho):
            order = sorted(range(1, count), key=lambda k: (-min(k, count - k), k))
            for k in order:
                for copy in copies(leg, rho, k, place[k], place[0], homes[k]):
                    copy.start()

        def arrive(leg, rho):
            for k in range(1, count):
                for copy in copies(leg, rho, k, place[0], place[count - k], homes[k]):
                    copy.wait_recv()

        def sent(leg, rho):
            for k in range(1, count):
                for copy in copies(leg, rho, k, place[k], place[0], homes[k]):
                    copy.wait_send()

        return start, arrive, sent

    _, x_arrive, x_sent = exchange(x_copies, x_to, x_home, 4)
    z_start, z_arrive, z_sent = exchange(z_copies, z_to, z_home, 16)

    def y_copies(leg, rho, k, h, frm, frm_core):
        to = y_to[k] * 2 + h
        send = 2 * k + h
        recv = 2 * k + frm_core
        return [
            remote(ysend_ref.at[leg, rho, to], yrecv_ref.at[leg, rho, frm], ys_sem.at[leg, rho, send], yr_sem.at[leg, rho, recv], y_home(k, h)),
            remote(ysc_ref.at[leg, rho, to], yscr_ref.at[leg, rho, frm], ycs_sem.at[leg, rho, send], ycr_sem.at[leg, rho, recv], y_home(k, h)),
        ]

    def y_partners(k):
        return (0, 1) if k else (1 - core,)

    def y_send(leg, rho, k):
        for h in y_partners(k):
            for copy in y_copies(leg, rho, k, h, q, core):
                copy.start()
        if k == 0:
            yrecv_ref[leg, rho, q] = ysend_ref[leg, rho, q]
            yscr_ref[leg, rho, q] = ysc_ref[leg, rho, q]

    def y_arrive(leg, rho):
        for k in (2, 1, 3, 0):
            for h in y_partners(k):
                for copy in y_copies(leg, rho, k, core, y_to[(4 - k) % 4] * 2 + h, h):
                    copy.wait_recv()

    def y_sent(leg, rho):
        for k in range(4):
            for h in y_partners(k):
                for copy in y_copies(leg, rho, k, h, q, core):
                    copy.wait_send()

    def x_send(leg, rho, k):
        if k:
            for copy in x_copies(leg, rho, k, x_to[k], x, x_home[k]):
                copy.start()
        else:
            xb_ref[leg, rho, :, x] = s16_ref[leg, rho, x]
            if leg == 1 or rho == 0:
                xsc_ref[leg, rho, x] = sc_ref[leg, rho, x]

    def z_phase(leg, rho):
        x_arrive(leg, rho)
        z_start(leg, rho)
        zb_ref[leg, rho, z] = xb_ref[leg, rho, z]
        if leg == 1 or rho == 0:
            zsc_ref[leg, rho, z] = xsc_ref[leg, rho]

    def operators(f):
        for b in range(NB):
            high, low = split(inv_ref[b, f].T)
            columns = slice(b % 2 * 128, b % 2 * 128 + 128)
            wc_ref[f, b // 2, 0:128, columns] = high
            wc_ref[f, b // 2, 128:256, columns] = high
            wc_ref[f, b // 2, 256:384, columns] = low

    def radial_forward(f):
        eye = lax.broadcasted_iota(jnp.int32, (32, 32), 0) == lax.broadcasted_iota(jnp.int32, (32, 32), 1)
        ones = jnp.ones((32, 128), BF16)
        largest = jnp.zeros((4, 128), F32)
        for rt in range(4):
            rows = slice(rt * 256, rt * 256 + 256)
            labels = bi_ref[rt * 8 : rt * 8 + 8, :].astype(F32)
            spread = [jnp.where(eye, jnp.broadcast_to(labels[t : t + 1], (32, 32)), 0.0) for t in range(8)]
            label = dot(jnp.concatenate(spread, axis=0).astype(BF16), ones)
            high, low = split(x_ref[f, rows, :])
            both = jnp.concatenate([high, low, high], axis=1)
            total = jnp.zeros((256, 128), F32)
            for b in range(0, NB, 2):
                pair = dot(both, wc_ref[f, b // 2])
                total = jnp.where(label == float(b), pair[:, :128], total)
                total = jnp.where(label == float(b + 1), pair[:, 128:], total)
            impl_ref[f, rows, :] = total
            high, low = split(total)
            grid = dot(cf_ref[...], jnp.concatenate([high, low, high], axis=1), ((1,), (1,)))
            for h in range(2):
                piece = grid[:, h * 128 : h * 128 + 128]
                s32_ref[f, pl.ds(rt * 2 + h, 128, stride=8), :] = piece
                largest = jnp.maximum(largest, jnp.max(jnp.abs(piece).reshape(4, 32, 128), axis=1))
        return largest

    for f in range(2):
        table_copies[f].wait()
    operators(0)
    operators(1)
    largest = radial_forward(0)

    pl.semaphore_wait(barrier, 25)

    fd16_ref[...] = fd_ref[...].astype(I16)
    quarter = pl.ds(pl.multiple_of(x * 256, 256), 256)

    def state_copy(k, to, frm):
        return remote(st_ref.at[:, pl.ds(2 * to, 2)], state_ref.at[frm], us_sem.at[k], ur_sem.at[k], l_home[k])

    def quarter_copy(k, frm):
        return remote(fd16_ref.at[:, quarter], fdall_ref.at[frm, :, quarter], fs_sem.at[k], fr_sem.at[k], l_home[k])

    def depth_copy(k, frm):
        part = pl.ds(pl.multiple_of(frm * 256, 256), 256)
        return remote(fdall_ref.at[:, :, part], fdall_ref.at[:, :, part], gs_sem.at[k], gr_sem.at[k], x_home[k])

    own_state = pltpu.make_async_copy(st_ref.at[:, pl.ds(2 * zl, 2)], state_ref.at[zl], own_sem)
    own_state.start()
    fdall_ref[zl, :, quarter] = fd16_ref[:, quarter]
    for k in (2, 1, 3):
        quarter_copy(k, zl).start()
        state_copy(k, l_to[k], zl).start()

    largest = jnp.maximum(jnp.maximum(largest, radial_forward(1)), 1e-30)
    inverse = QMAX / largest
    scale = largest * (1.0 / QMAX)
    for xx in range(4):
        sc_ref[0, 0, xx] = scale[xx : xx + 1]
        for rho in range(2):
            both = [
                s32_ref[f, xx * 256 : xx * 256 + 256, :].reshape(16, 2, 8, 128)[:, rho] for f in range(2)
            ]
            s16_ref[0, rho, xx] = quantize(jnp.concatenate(both, axis=1), inverse[xx : xx + 1])

    for rho in range(2):
        for k in (2, 1, 3, 0):
            x_send(0, rho, k)
    z_phase(0, 0)
    z_phase(0, 1)

    for copy in table_copies[2:]:
        copy.wait()

    def keep_columns(par, rows, f, value):
        high, low = split(value)
        start, size = rows
        columns = slice(f * 128, f * 128 + 128)
        xcat_ref[par, pl.ds(start, size), columns] = high
        xcat_ref[par, pl.ds(256 + start, size), columns] = low
        xcat_ref[par, pl.ds(512 + start, size), columns] = high

    def send_block(leg, rho, p, fields):
        most = jnp.maximum(jnp.abs(fields[0]), jnp.abs(fields[1]))
        most = jnp.maximum(jnp.max(most, axis=0, keepdims=True), 1e-30)
        inverse = QMAX / most
        ysc_ref[leg, rho, p] = most * (1.0 / QMAX)
        for f in range(2):
            ysend_ref[leg, rho, p, f] = quantize(fields[f], inverse)

    def theta_forward(rho):
        z_arrive(0, rho)

        def body(xx, carry):
            for zh in range(4):
                tiles = [
                    restore(zb_ref[0, rho, zh * 4 + s, xx], zsc_ref[0, 0, zh * 4 + s, xx]) for s in range(4)
                ]
                tiles = swap_groups(tiles)
                start = pl.multiple_of(xx * 64 + zh * 16, 16)
                for f in range(2):
                    for par in range(2):
                        rows = jnp.concatenate([tile[f * 8 : f * 8 + 8] for tile in tiles[par::2]], axis=0)
                        keep_columns(par, (start, 16), f, rows)
            return carry

        lax.fori_loop(0, 4, body, 0)
        evens = dot(tf_ref[0], xcat_ref[0])
        odds = dot(tf_ref[1], xcat_ref[1])
        t32_ref[0] = evens + odds
        t32_ref[1] = evens - odds
        for k in (2, 1, 3, 0):
            for h in range(2):
                p = y_to[k] * 2 + h
                rows = pl.ds(pl.multiple_of(p * 32, 32), 32)
                grid = jnp.concatenate([t32_ref[0, rows, :], t32_ref[1, rows, :]], axis=0)
                send_block(0, rho, p, [grid[:, f * 128 : f * 128 + 128] for f in range(2)])
            y_send(0, rho, k)

    def axial_forward(rho):
        y_arrive(0, rho)
        for m in range(4):
            lanes = slice(m * 128, m * 128 + 128)
            for f in range(2):
                pair = swap_parity(*[restore(yrecv_ref[0, rho, p, f], yscr_ref[0, rho, p]) for p in (2 * m, 2 * m + 1)])
                for par in range(2):
                    high, low = split(pair[par])
                    a_ref[par, f * 64 : f * 64 + 64, lanes] = high
                    a_ref[par, 128 + f * 64 : 128 + f * 64 + 64, lanes] = low

        def force(grid, columns):
            keep = keep_ref[rho, :, columns]
            u0 = jnp.concatenate([state_ref[s, 0, rho, :, columns] for s in range(4)], axis=0).astype(F32)
            u1 = jnp.concatenate([state_ref[s, 1, rho, :, columns] for s in range(4)], axis=0).astype(F32)
            g0 = grid[:64]
            g1 = grid[64:]
            pull = tang_ref[rho, :, columns] * (u0 * g0 + u1 * g1)
            return jnp.concatenate([pull * u0 - keep * g0, pull * u1 - keep * g1], axis=0)

        for n in range(2):
            columns = slice(n * 256, n * 256 + 256)
            sums = []
            for par in range(2):
                twice = dot(a_ref[par], wh_ref[par, :, columns])
                sums.append(twice[:128] + twice[128:] + dot(a_ref[par, :128], wl_ref[par, :, columns]))
            lower = force(sums[0] + sums[1], columns)
            upper = force(sums[0] - sums[1], slice(512 + n * 256, 512 + n * 256 + 256))
            for par, value in enumerate((lower + upper, lower - upper)):
                high, low = split(value)
                f_ref[par, :128, columns] = high
                f_ref[par, 128:, columns] = low

    def axial_back(rho):
        own_half = lax.div(y, 2)
        for i in range(2):
            n = own_half if i else 1 - own_half
            columns = pl.ds(pl.multiple_of(n * 256, 256), 256)
            modes = []
            for par in range(2):
                twice = dot(f_ref[par], vh_ref[par, :, columns])
                modes.append(twice[:128] + twice[128:] + dot(f_ref[par, :128], vl_ref[par, :, columns]))
            for m in range(2):
                lanes = slice(m * 128, m * 128 + 128)
                blocks = swap_parity(modes[0][:, lanes], modes[1][:, lanes])
                for h in range(2):
                    send_block(1, rho, n * 4 + m * 2 + h, [blocks[h][f * 64 : f * 64 + 64] for f in range(2)])
            for k in (1, 3, 0) if i else (2,):
                y_send(1, rho, k)

    def theta_back(rho):
        y_arrive(1, rho)
        for p in range(8):
            for f in range(2):
                grid = restore(yrecv_ref[1, rho, p, f], yscr_ref[1, rho, p])
                keep_columns(0, (p * 32, 32), f, grid[:32] + grid[32:])
                keep_columns(1, (p * 32, 32), f, grid[:32] - grid[32:])
        for par in range(2):
            t32_ref[par] = dot(tb_ref[par], xcat_ref[par])
        for k in (2, 1, 3, 0):
            xx = x_to[k]
            rows = pl.ds(pl.multiple_of(xx * 64, 64), 64)
            modes = [t32_ref[par, rows, :] for par in range(2)]
            tiles = []
            for n in range(4):
                tiles += swap_groups([
                    jnp.concatenate(
                        [
                            modes[a % 2][n * 16 + a // 2 * 8 : n * 16 + a // 2 * 8 + 8, f * 128 : f * 128 + 128]
                            for f in range(2)
                        ],
                        axis=0,
                    )
                    for a in range(4)
                ])
            most = jnp.abs(tiles[0])
            for tile in tiles[1:]:
                most = jnp.maximum(most, jnp.abs(tile))
            most = jnp.maximum(jnp.max(most, axis=0, keepdims=True), 1e-30)
            inverse = QMAX / most
            sc_ref[1, rho, xx] = most * (1.0 / QMAX)
            for n in range(16):
                s16_ref[1, rho, xx, n] = quantize(tiles[n], inverse)
            x_send(1, rho, k)

    theta_forward(0)

    for k in range(1, 4):
        quarter_copy(k, l_to[4 - k]).wait_recv()
    for k in range(1, 4):
        depth_copy(k, x).start()

    for k in range(1, 4):
        state_copy(k, zl, l_to[4 - k]).wait_recv()
        depth_copy(k, x_to[4 - k]).wait_recv()
    own_state.wait()
    for rho in range(2):
        for s in range(4):
            u0 = state_ref[s, 0, rho].astype(F32)
            u1 = state_ref[s, 1, rho].astype(F32)
            root = lax.rsqrt(1.0 + (u0 * u0 + u1 * u1))
            viscosity = root * lax.rsqrt(root)
            depth = fdall_ref[s].astype(jnp.int32)
            frozen = jnp.where(2 * group + rho >= R - depth, penalty, 0.0)
            keep_ref[rho, s * 16 : s * 16 + 16] = viscosity + frozen
            tang_ref[rho, s * 16 : s * 16 + 16] = 0.5 * viscosity * (root * root)

    axial_forward(0)
    axial_back(0)
    theta_forward(1)
    theta_back(0)
    axial_forward(1)
    z_phase(1, 0)
    axial_back(1)
    theta_back(1)
    z_phase(1, 1)

    for leg, rho in ((0, 0), (0, 1), (1, 0)):
        x_sent(leg, rho)
        z_sent(leg, rho)
        y_sent(leg, rho)
    x_sent(1, 1)
    y_sent(1, 1)
    for k in range(1, 4):
        state_copy(k, l_to[k], zl).wait_send()
        quarter_copy(k, zl).wait_send()
        depth_copy(k, x).wait_send()
    for rho in range(2):
        z_arrive(1, rho)
        for xx in range(4):
            tile = restore(zb_ref[1, rho, :, xx], zsc_ref[1, rho, :, xx])
            for f in range(2):
                d32_ref[f, xx * 128 : xx * 128 + 128, :] = tile[:, f * 8 : f * 8 + 8].reshape(128, 128)
        for f in range(2):
            for tg in range(8):
                high, low = split(d32_ref[f, pl.ds(tg, 64, stride=8), :])
                gamma = dot(jnp.concatenate([high, low, high], axis=0), cb_ref[rho], ((0,), (0,)))
                rows = slice(tg * 128, tg * 128 + 128)
                before = impl_ref if rho == 0 else out_ref
                out_ref[f, rows, :] = before[f, rows, :] + step_dt * gamma
    z_sent(1, 1)


def on_device(adj_coef, grid_state, block_index, frozen_depth, inv_blocks):
    constants = [jnp.asarray(table) for table in tables()]
    vmem = pl.BlockSpec(memory_space=pltpu.VMEM)
    hbm = pl.BlockSpec(memory_space=pltpu.HBM)
    dma = pltpu.SemaphoreType.DMA
    scratch = [
        pltpu.VMEM((2, 1024, 128), F32),
        pltpu.VMEM((NB, 2, 128, 128), F32),
        pltpu.VMEM((2, 256, 768), BF16),
        pltpu.VMEM((2, 256, 768), BF16),
        pltpu.VMEM((2, NZ // 2, NZ // 2), BF16),
        pltpu.VMEM((2, NZ // 2, NZ // 2), BF16),
        pltpu.VMEM((2, NZ // 2, NZ // 2), BF16),
        pltpu.VMEM((2, NZ // 2, NZ // 2), BF16),
        pltpu.VMEM((2, NB // 2, 384, 256), BF16),
        pltpu.VMEM((2, 1024, 128), F32),
        pltpu.VMEM((2, 1024, 128), F32),
        pltpu.VMEM((2, 512, 128), F32),
        pltpu.VMEM((2, 2, 4, 16, 16, 128), I16),
        pltpu.VMEM((2, 2, 16, 4, 16, 128), I16),
        pltpu.VMEM((2, 2, 16, 4, 16, 128), I16),
        pltpu.VMEM((2, 2, 4, 1, 128), F32),
        pltpu.VMEM((2, 2, 4, 1, 128), F32),
        pltpu.VMEM((2, 2, 16, 4, 1, 128), F32),
        pltpu.VMEM((2, 2, 8, 2, 64, 128), I16),
        pltpu.VMEM((2, 2, 8, 2, 64, 128), I16),
        pltpu.VMEM((2, 2, 8, 1, 128), F32),
        pltpu.VMEM((2, 2, 8, 1, 128), F32),
        pltpu.VMEM((4, 2, 2, 16, NZ), BF16),
        pltpu.VMEM((16, NZ), I16),
        pltpu.VMEM((4, 16, NZ), I16),
        pltpu.VMEM((2, 64, NZ), F32),
        pltpu.VMEM((2, 64, NZ), F32),
        pltpu.VMEM((2, 768, 256), BF16),
        pltpu.VMEM((2, 256, NZ // 2), BF16),
        pltpu.VMEM((2, 256, NZ // 2), BF16),
        pltpu.VMEM((2, 256, 256), F32),
        dma((8,)),
        dma((2, 2, 4)), dma((2, 2, 4)), dma((2, 2, 16)), dma((2, 2, 16)), dma((2, 2, 8)), dma((2, 2, 8)),
        dma((2, 2, 4)), dma((2, 2, 4)), dma((2, 2, 16)), dma((2, 2, 16)), dma((2, 2, 8)), dma((2, 2, 8)),
        dma((4,)), dma((4,)), dma((4,)), dma((4,)), dma((4,)), dma((4,)), dma,
    ]
    step = pl.pallas_call(
        kernel,
        out_shape=jax.ShapeDtypeStruct((2, 1024, R), F32),
        in_specs=[hbm, hbm, vmem, vmem, hbm, vmem, vmem] + [hbm] * 6,
        out_specs=vmem,
        scratch_shapes=scratch,
        compiler_params=pltpu.CompilerParams(
            collective_id=0, has_side_effects=True, vmem_limit_bytes=56 * 1024 * 1024
        ),
    )
    flat = adj_coef.reshape(2, 1024, R)
    result = step(flat, grid_state, block_index, frozen_depth, inv_blocks, *constants)
    return result.reshape(2, 32, 32, R)


def solution(mesh):
    placed = (
        P(None, "az", "ax", None),
        P(None, "az", "ax", None),
        P("az", "ax"),
        P("ax", None),
        P(),
    )
    return jax.shard_map(
        on_device, mesh=mesh, in_specs=placed, out_specs=P(None, "az", "ax", None), check_vma=False
    )
```

```python
import math

import jax
import jax.numpy as jnp
import ml_dtypes
import numpy as np
from jax import lax
from jax.experimental import pallas as pl
from jax.experimental.pallas import tpu as pltpu
from jax.sharding import PartitionSpec as P

NT = 512
NZ = 1024
R = 128
NB = 8
penalty = 2.0
step_dt = 0.3
QMAX = 32767.0
ROUNDER = 12582912.0
F32 = jnp.float32
BF16 = jnp.bfloat16
I16 = jnp.int16
MESH = pl.DeviceIdType.MESH


def hartley(count):
    index = np.arange(count, dtype=np.int64)
    angle = (index[:, None] * index[None, :] % count) * (2.0 * math.pi / count)
    return (np.cos(angle) + np.sin(angle)) / math.sqrt(count)


def chebyshev(count):
    index = np.arange(count, dtype=np.int64)
    angle = (index[:, None] * index[None, :] % (2 * (count - 1))) * (math.pi / (count - 1))
    return np.cos(angle) * math.sqrt(2.0 / count)


def parts(table):
    high = table.astype(ml_dtypes.bfloat16)
    low = (table - high.astype(np.float64)).astype(ml_dtypes.bfloat16)
    return high, low


def tables():
    q, zl, i = np.meshgrid(np.arange(8), np.arange(2), np.arange(16), indexing="ij")
    theta_order = (16 * (zl * 8 + q) + i).reshape(-1)
    az, half, tg = np.meshgrid(np.arange(16), np.arange(2), np.arange(8), indexing="ij")
    mode_order = (32 * az + tg * 4 + 2 * half).reshape(-1)
    pair, lane = np.meshgrid(np.arange(4), np.arange(128), indexing="ij")
    device = 2 * pair + lane % 2
    axial_order = (32 * (lane // 32 * 8 + device) + lane % 32 // 2 * 2).reshape(-1)
    theta_full = hartley(NT)[theta_order]
    theta = np.stack([theta_full[:, mode_order + par] for par in range(2)])
    axial = np.stack([hartley(NZ)[axial_order + par][:, : NZ // 2] for par in range(2)])
    radial = chebyshev(R)
    ch, cl = parts(radial)
    dh, dl = parts(np.stack([radial[0::2], radial[1::2]]))
    th, tl = parts(theta)
    bh, bl = parts(theta.transpose(0, 2, 1))
    wh, wl = parts(axial)
    vh, vl = parts(np.ascontiguousarray(axial.transpose(0, 2, 1)))
    return [
        np.concatenate([ch, ch, cl], axis=1),
        np.stack([np.concatenate([dh[i], dh[i], dl[i]], axis=0) for i in range(2)]),
        np.concatenate([th, th, tl], axis=2),
        np.concatenate([bh, bh, bl], axis=2),
        wh,
        wl,
        vh,
        vl,
    ]


def split(value):
    high = value.astype(BF16)
    low = (value - high.astype(F32)).astype(BF16)
    return high, low


def dot(a, b, dims=((1,), (0,))):
    return lax.dot_general(a, b, (dims, ((), ())), preferred_element_type=F32)


def swap_groups(tiles):
    lane = lax.broadcasted_iota(jnp.int32, tiles[0].shape, 1)
    first = lane < 64
    even = lane % 64 < 32
    t0, t1, t2, t3 = tiles
    a0 = jnp.where(first, t0, pltpu.roll(t2, 64, 1))
    a2 = jnp.where(first, pltpu.roll(t0, 64, 1), t2)
    a1 = jnp.where(first, t1, pltpu.roll(t3, 64, 1))
    a3 = jnp.where(first, pltpu.roll(t1, 64, 1), t3)
    b0 = jnp.where(even, a0, pltpu.roll(a1, 32, 1))
    b1 = jnp.where(even, pltpu.roll(a0, 96, 1), a1)
    b2 = jnp.where(even, a2, pltpu.roll(a3, 32, 1))
    b3 = jnp.where(even, pltpu.roll(a2, 96, 1), a3)
    return [b0, b1, b2, b3]


def swap_parity(first, second):
    even = lax.broadcasted_iota(jnp.int32, first.shape, 1) % 2 == 0
    return (
        jnp.where(even, first, pltpu.roll(second, 1, 1)),
        jnp.where(even, pltpu.roll(first, 127, 1), second),
    )


def quantize(value, inverse):
    whole = (value * inverse + ROUNDER) - ROUNDER
    return whole.astype(jnp.int32).astype(I16)


def restore(value, scale):
    return value.astype(jnp.int32).astype(F32) * scale


def kernel(
    x_in, st_ref, bi_ref, fd_ref, inv_in, cf_ref, cb_ref,
    tf_in, tb_in, wh_in, wl_in, vh_in, vl_in,
    out_ref,
    x_ref, inv_ref, tf_ref, tb_ref, wh_ref, wl_ref, vh_ref, vl_ref,
    wc_ref, impl_ref, s32_ref, d32_ref,
    s16_ref, xb_ref, zb_ref, sc_ref, xsc_ref, zsc_ref,
    ysend_ref, yrecv_ref, ysc_ref, yscr_ref,
    state_ref, fd16_ref, fdall_ref, keep_ref, tang_ref,
    xcat_ref, a_ref, f_ref, t32_ref,
    table_sem, xs_sem, xr_sem, zs_sem, zr_sem, ys_sem, yr_sem,
    xcs_sem, xcr_sem, zcs_sem, zcr_sem, ycs_sem, ycr_sem,
    us_sem, ur_sem, fs_sem, fr_sem, gs_sem, gr_sem, own_sem,
):
    az = lax.axis_index("az")
    ax = lax.axis_index("ax")
    x = lax.div(az, 4)
    zl = lax.div(ax, 8)
    q = lax.rem(ax, 8)
    y = lax.div(q, 2)
    core = lax.rem(q, 2)
    z = lax.rem(az, 4) * 4 + zl
    group = x * 16 + z

    x_to = [lax.rem(x + k, 4) for k in range(4)]
    z_to = [lax.rem(z + k, 16) for k in range(16)]
    x_home = [(xx * 4 + lax.rem(az, 4), ax) for xx in x_to]
    z_home = [(x * 4 + lax.div(zz, 4), lax.rem(zz, 4) * 8 + q) for zz in z_to]
    y_to = [lax.rem(y + k, 4) for k in range(4)]
    l_to = [lax.rem(zl + k, 4) for k in range(4)]
    l_home = [(az, ll * 8 + q) for ll in l_to]

    def y_home(k, h):
        return (az, zl * 8 + y_to[k] * 2 + h)

    def remote(src, dst, send, recv, device):
        return pltpu.make_async_remote_copy(
            src_ref=src, dst_ref=dst, send_sem=send, recv_sem=recv, device_id=device, device_id_type=MESH
        )

    table_copies = [
        pltpu.make_async_copy(src, dst, table_sem.at[n])
        for n, (src, dst) in enumerate(
            [
                (inv_in, inv_ref), (x_in, x_ref), (tf_in, tf_ref), (tb_in, tb_ref),
                (wh_in, wh_ref), (wl_in, wl_ref), (vh_in, vh_ref), (vl_in, vl_ref),
            ]
        )
    ]
    for copy in table_copies:
        copy.start()
    barrier = pltpu.get_barrier_semaphore()
    homes = x_home[1:] + z_home[1:] + [y_home(k, h) for k in range(1, 4) for h in range(2)] + [y_home(0, 1 - core)]
    for home in homes:
        pl.semaphore_signal(barrier, inc=1, device_id=home, device_id_type=MESH)

    def x_copies(leg, rho, k, to, frm, home):
        data = [
            remote(s16_ref.at[leg, rho, to], xb_ref.at[leg, rho, :, frm], xs_sem.at[leg, rho, k], xr_sem.at[leg, rho, k], home),
        ]
        if leg == 0 and rho == 1:
            return data
        return data + [
            remote(sc_ref.at[leg, rho, to], xsc_ref.at[leg, rho, frm], xcs_sem.at[leg, rho, k], xcr_sem.at[leg, rho, k], home),
        ]

    def z_copies(leg, rho, k, to, frm, home):
        data = [
            remote(xb_ref.at[leg, rho, to], zb_ref.at[leg, rho, frm], zs_sem.at[leg, rho, k], zr_sem.at[leg, rho, k], home),
        ]
        if leg == 0 and rho == 1:
            return data
        return data + [
            remote(xsc_ref.at[leg, rho], zsc_ref.at[leg, rho, frm], zcs_sem.at[leg, rho, k], zcr_sem.at[leg, rho, k], home),
        ]

    def exchange(copies, place, homes, count):
        def start(leg, rho):
            order = sorted(range(1, count), key=lambda k: (-min(k, count - k), k))
            for k in order:
                for copy in copies(leg, rho, k, place[k], place[0], homes[k]):
                    copy.start()

        def arrive(leg, rho):
            for k in range(1, count):
                for copy in copies(leg, rho, k, place[0], place[count - k], homes[k]):
                    copy.wait_recv()

        def sent(leg, rho):
            for k in range(1, count):
                for copy in copies(leg, rho, k, place[k], place[0], homes[k]):
                    copy.wait_send()

        return start, arrive, sent

    _, x_arrive, x_sent = exchange(x_copies, x_to, x_home, 4)
    z_start, z_arrive, z_sent = exchange(z_copies, z_to, z_home, 16)

    def y_copies(leg, rho, k, h, frm, frm_core):
        to = y_to[k] * 2 + h
        send = 2 * k + h
        recv = 2 * k + frm_core
        return [
            remote(ysend_ref.at[leg, rho, to], yrecv_ref.at[leg, rho, frm], ys_sem.at[leg, rho, send], yr_sem.at[leg, rho, recv], y_home(k, h)),
            remote(ysc_ref.at[leg, rho, to], yscr_ref.at[leg, rho, frm], ycs_sem.at[leg, rho, send], ycr_sem.at[leg, rho, recv], y_home(k, h)),
        ]

    def y_partners(k):
        return (0, 1) if k else (1 - core,)

    def y_send(leg, rho, k):
        for h in y_partners(k):
            for copy in y_copies(leg, rho, k, h, q, core):
                copy.start()
        if k == 0:
            yrecv_ref[leg, rho, q] = ysend_ref[leg, rho, q]
            yscr_ref[leg, rho, q] = ysc_ref[leg, rho, q]

    def y_arrive(leg, rho):
        for k in (2, 1, 3, 0):
            for h in y_partners(k):
                for copy in y_copies(leg, rho, k, core, y_to[(4 - k) % 4] * 2 + h, h):
                    copy.wait_recv()

    def y_sent(leg, rho):
        for k in range(4):
            for h in y_partners(k):
                for copy in y_copies(leg, rho, k, h, q, core):
                    copy.wait_send()

    def x_send(leg, rho, k):
        if k:
            for copy in x_copies(leg, rho, k, x_to[k], x, x_home[k]):
                copy.start()
        else:
            xb_ref[leg, rho, :, x] = s16_ref[leg, rho, x]
            if leg == 1 or rho == 0:
                xsc_ref[leg, rho, x] = sc_ref[leg, rho, x]

    def z_phase(leg, rho):
        x_arrive(leg, rho)
        z_start(leg, rho)
        zb_ref[leg, rho, z] = xb_ref[leg, rho, z]
        if leg == 1 or rho == 0:
            zsc_ref[leg, rho, z] = xsc_ref[leg, rho]

    def operators(f):
        for b in range(NB):
            high, low = split(inv_ref[b, f].T)
            columns = slice(b % 2 * 128, b % 2 * 128 + 128)
            wc_ref[f, b // 2, 0:128, columns] = high
            wc_ref[f, b // 2, 128:256, columns] = high
            wc_ref[f, b // 2, 256:384, columns] = low

    def radial_forward(f):
        eye = lax.broadcasted_iota(jnp.int32, (32, 32), 0) == lax.broadcasted_iota(jnp.int32, (32, 32), 1)
        ones = jnp.ones((32, 128), BF16)
        largest = jnp.zeros((4, 128), F32)
        for rt in range(4):
            rows = slice(rt * 256, rt * 256 + 256)
            labels = bi_ref[rt * 8 : rt * 8 + 8, :].astype(F32)
            spread = [jnp.where(eye, jnp.broadcast_to(labels[t : t + 1], (32, 32)), 0.0) for t in range(8)]
            label = dot(jnp.concatenate(spread, axis=0).astype(BF16), ones)
            high, low = split(x_ref[f, rows, :])
            both = jnp.concatenate([high, low, high], axis=1)
            total = jnp.zeros((256, 128), F32)
            for b in range(0, NB, 2):
                pair = dot(both, wc_ref[f, b // 2])
                total = jnp.where(label == float(b), pair[:, :128], total)
                total = jnp.where(label == float(b + 1), pair[:, 128:], total)
            impl_ref[f, rows, :] = total
            high, low = split(total)
            grid = dot(cf_ref[...], jnp.concatenate([high, low, high], axis=1), ((1,), (1,)))
            for h in range(2):
                piece = grid[:, h * 128 : h * 128 + 128]
                s32_ref[f, pl.ds(rt * 2 + h, 128, stride=8), :] = piece
                largest = jnp.maximum(largest, jnp.max(jnp.abs(piece).reshape(4, 32, 128), axis=1))
        return largest

    for f in range(2):
        table_copies[f].wait()
    operators(0)
    operators(1)
    largest = jnp.maximum(jnp.maximum(radial_forward(0), radial_forward(1)), 1e-30)
    inverse = QMAX / largest
    scale = largest * (1.0 / QMAX)
    for xx in range(4):
        sc_ref[0, 0, xx] = scale[xx : xx + 1]

    def code(rho):
        for xx in range(4):
            both = [
                s32_ref[f, xx * 256 : xx * 256 + 256, :].reshape(16, 2, 8, 128)[:, rho] for f in range(2)
            ]
            s16_ref[0, rho, xx] = quantize(jnp.concatenate(both, axis=1), inverse[xx : xx + 1])

    code(0)

    pl.semaphore_wait(barrier, 25)
    for k in (2, 1, 3, 0):
        x_send(0, 0, k)
    code(1)
    for k in (2, 1, 3, 0):
        x_send(0, 1, k)

    fd16_ref[...] = fd_ref[...].astype(I16)
    quarter = pl.ds(pl.multiple_of(x * 256, 256), 256)

    def state_copy(k, to, frm):
        return remote(st_ref.at[:, pl.ds(2 * to, 2)], state_ref.at[frm], us_sem.at[k], ur_sem.at[k], l_home[k])

    def quarter_copy(k, frm):
        return remote(fd16_ref.at[:, quarter], fdall_ref.at[frm, :, quarter], fs_sem.at[k], fr_sem.at[k], l_home[k])

    def depth_copy(k, frm):
        part = pl.ds(pl.multiple_of(frm * 256, 256), 256)
        return remote(fdall_ref.at[:, :, part], fdall_ref.at[:, :, part], gs_sem.at[k], gr_sem.at[k], x_home[k])

    own_state = pltpu.make_async_copy(st_ref.at[:, pl.ds(2 * zl, 2)], state_ref.at[zl], own_sem)
    own_state.start()
    fdall_ref[zl, :, quarter] = fd16_ref[:, quarter]
    z_phase(0, 0)
    for k in (2, 1, 3):
        quarter_copy(k, zl).start()
        state_copy(k, l_to[k], zl).start()
    z_phase(0, 1)

    for copy in table_copies[2:]:
        copy.wait()

    def keep_columns(par, rows, f, value):
        high, low = split(value)
        start, size = rows
        columns = slice(f * 128, f * 128 + 128)
        xcat_ref[par, pl.ds(start, size), columns] = high
        xcat_ref[par, pl.ds(256 + start, size), columns] = low
        xcat_ref[par, pl.ds(512 + start, size), columns] = high

    def send_block(leg, rho, p, fields):
        most = jnp.maximum(jnp.abs(fields[0]), jnp.abs(fields[1]))
        most = jnp.maximum(jnp.max(most, axis=0, keepdims=True), 1e-30)
        inverse = QMAX / most
        ysc_ref[leg, rho, p] = most * (1.0 / QMAX)
        for f in range(2):
            ysend_ref[leg, rho, p, f] = quantize(fields[f], inverse)

    def theta_forward(rho):
        z_arrive(0, rho)

        def body(xx, carry):
            for zh in range(4):
                tiles = [
                    restore(zb_ref[0, rho, zh * 4 + s, xx], zsc_ref[0, 0, zh * 4 + s, xx]) for s in range(4)
                ]
                tiles = swap_groups(tiles)
                start = pl.multiple_of(xx * 64 + zh * 16, 16)
                for f in range(2):
                    for par in range(2):
                        rows = jnp.concatenate([tile[f * 8 : f * 8 + 8] for tile in tiles[par::2]], axis=0)
                        keep_columns(par, (start, 16), f, rows)
            return carry

        lax.fori_loop(0, 4, body, 0)
        evens = dot(tf_ref[0], xcat_ref[0])
        odds = dot(tf_ref[1], xcat_ref[1])
        t32_ref[0] = evens + odds
        t32_ref[1] = evens - odds
        for k in (2, 1, 3, 0):
            for h in range(2):
                p = y_to[k] * 2 + h
                rows = pl.ds(pl.multiple_of(p * 32, 32), 32)
                grid = jnp.concatenate([t32_ref[0, rows, :], t32_ref[1, rows, :]], axis=0)
                send_block(0, rho, p, [grid[:, f * 128 : f * 128 + 128] for f in range(2)])
            y_send(0, rho, k)

    def axial_forward(rho):
        y_arrive(0, rho)
        for m in range(4):
            lanes = slice(m * 128, m * 128 + 128)
            for f in range(2):
                pair = swap_parity(*[restore(yrecv_ref[0, rho, p, f], yscr_ref[0, rho, p]) for p in (2 * m, 2 * m + 1)])
                for par in range(2):
                    high, low = split(pair[par])
                    a_ref[par, f * 64 : f * 64 + 64, lanes] = high
                    a_ref[par, 128 + f * 64 : 128 + f * 64 + 64, lanes] = low

        def force(grid, columns):
            keep = keep_ref[rho, :, columns]
            u0 = jnp.concatenate([state_ref[s, 0, rho, :, columns] for s in range(4)], axis=0).astype(F32)
            u1 = jnp.concatenate([state_ref[s, 1, rho, :, columns] for s in range(4)], axis=0).astype(F32)
            g0 = grid[:64]
            g1 = grid[64:]
            pull = tang_ref[rho, :, columns] * (u0 * g0 + u1 * g1)
            return jnp.concatenate([pull * u0 - keep * g0, pull * u1 - keep * g1], axis=0)

        for n in range(2):
            columns = slice(n * 256, n * 256 + 256)
            sums = []
            for par in range(2):
                twice = dot(a_ref[par], wh_ref[par, :, columns])
                sums.append(twice[:128] + twice[128:] + dot(a_ref[par, :128], wl_ref[par, :, columns]))
            lower = force(sums[0] + sums[1], columns)
            upper = force(sums[0] - sums[1], slice(512 + n * 256, 512 + n * 256 + 256))
            for par, value in enumerate((lower + upper, lower - upper)):
                high, low = split(value)
                f_ref[par, :128, columns] = high
                f_ref[par, 128:, columns] = low

    def axial_back(rho):
        own_half = lax.div(y, 2)
        for i in range(2):
            n = own_half if i else 1 - own_half
            columns = pl.ds(pl.multiple_of(n * 256, 256), 256)
            modes = []
            for par in range(2):
                twice = dot(f_ref[par], vh_ref[par, :, columns])
                modes.append(twice[:128] + twice[128:] + dot(f_ref[par, :128], vl_ref[par, :, columns]))
            for m in range(2):
                lanes = slice(m * 128, m * 128 + 128)
                blocks = swap_parity(modes[0][:, lanes], modes[1][:, lanes])
                for h in range(2):
                    send_block(1, rho, n * 4 + m * 2 + h, [blocks[h][f * 64 : f * 64 + 64] for f in range(2)])
            for k in (1, 3, 0) if i else (2,):
                y_send(1, rho, k)

    def theta_back(rho):
        y_arrive(1, rho)
        for p in range(8):
            for f in range(2):
                grid = restore(yrecv_ref[1, rho, p, f], yscr_ref[1, rho, p])
                keep_columns(0, (p * 32, 32), f, grid[:32] + grid[32:])
                keep_columns(1, (p * 32, 32), f, grid[:32] - grid[32:])
        for par in range(2):
            t32_ref[par] = dot(tb_ref[par], xcat_ref[par])
        for k in (2, 1, 3, 0):
            xx = x_to[k]
            rows = pl.ds(pl.multiple_of(xx * 64, 64), 64)
            modes = [t32_ref[par, rows, :] for par in range(2)]
            tiles = []
            for n in range(4):
                tiles += swap_groups([
                    jnp.concatenate(
                        [
                            modes[a % 2][n * 16 + a // 2 * 8 : n * 16 + a // 2 * 8 + 8, f * 128 : f * 128 + 128]
                            for f in range(2)
                        ],
                        axis=0,
                    )
                    for a in range(4)
                ])
            most = jnp.abs(tiles[0])
            for tile in tiles[1:]:
                most = jnp.maximum(most, jnp.abs(tile))
            most = jnp.maximum(jnp.max(most, axis=0, keepdims=True), 1e-30)
            inverse = QMAX / most
            sc_ref[1, rho, xx] = most * (1.0 / QMAX)
            for n in range(16):
                s16_ref[1, rho, xx, n] = quantize(tiles[n], inverse)
            x_send(1, rho, k)

    theta_forward(0)

    for k in range(1, 4):
        quarter_copy(k, l_to[4 - k]).wait_recv()
    for k in range(1, 4):
        depth_copy(k, x).start()

    for k in range(1, 4):
        state_copy(k, zl, l_to[4 - k]).wait_recv()
        depth_copy(k, x_to[4 - k]).wait_recv()
    own_state.wait()
    for rho in range(2):
        for s in range(4):
            u0 = state_ref[s, 0, rho].astype(F32)
            u1 = state_ref[s, 1, rho].astype(F32)
            root = lax.rsqrt(1.0 + (u0 * u0 + u1 * u1))
            viscosity = root * lax.rsqrt(root)
            depth = fdall_ref[s].astype(jnp.int32)
            frozen = jnp.where(2 * group + rho >= R - depth, penalty, 0.0)
            keep_ref[rho, s * 16 : s * 16 + 16] = viscosity + frozen
            tang_ref[rho, s * 16 : s * 16 + 16] = 0.5 * viscosity * (root * root)

    axial_forward(0)
    axial_back(0)
    theta_forward(1)
    theta_back(0)
    axial_forward(1)
    axial_back(1)
    z_phase(1, 0)
    theta_back(1)
    z_phase(1, 1)

    for leg, rho in ((0, 0), (0, 1), (1, 0)):
        x_sent(leg, rho)
        z_sent(leg, rho)
        y_sent(leg, rho)
    x_sent(1, 1)
    y_sent(1, 1)
    for k in range(1, 4):
        state_copy(k, l_to[k], zl).wait_send()
        quarter_copy(k, zl).wait_send()
        depth_copy(k, x).wait_send()
    for rho in range(2):
        z_arrive(1, rho)
        for xx in range(4):
            tile = restore(zb_ref[1, rho, :, xx], zsc_ref[1, rho, :, xx])
            for f in range(2):
                d32_ref[f, xx * 128 : xx * 128 + 128, :] = tile[:, f * 8 : f * 8 + 8].reshape(128, 128)
        for f in range(2):
            for tg in range(8):
                high, low = split(d32_ref[f, pl.ds(tg, 64, stride=8), :])
                gamma = dot(jnp.concatenate([high, low, high], axis=0), cb_ref[rho], ((0,), (0,)))
                rows = slice(tg * 128, tg * 128 + 128)
                before = impl_ref if rho == 0 else out_ref
                out_ref[f, rows, :] = before[f, rows, :] + step_dt * gamma
    z_sent(1, 1)


def on_device(adj_coef, grid_state, block_index, frozen_depth, inv_blocks):
    constants = [jnp.asarray(table) for table in tables()]
    vmem = pl.BlockSpec(memory_space=pltpu.VMEM)
    hbm = pl.BlockSpec(memory_space=pltpu.HBM)
    dma = pltpu.SemaphoreType.DMA
    scratch = [
        pltpu.VMEM((2, 1024, 128), F32),
        pltpu.VMEM((NB, 2, 128, 128), F32),
        pltpu.VMEM((2, 256, 768), BF16),
        pltpu.VMEM((2, 256, 768), BF16),
        pltpu.VMEM((2, NZ // 2, NZ // 2), BF16),
        pltpu.VMEM((2, NZ // 2, NZ // 2), BF16),
        pltpu.VMEM((2, NZ // 2, NZ // 2), BF16),
        pltpu.VMEM((2, NZ // 2, NZ // 2), BF16),
        pltpu.VMEM((2, NB // 2, 384, 256), BF16),
        pltpu.VMEM((2, 1024, 128), F32),
        pltpu.VMEM((2, 1024, 128), F32),
        pltpu.VMEM((2, 512, 128), F32),
        pltpu.VMEM((2, 2, 4, 16, 16, 128), I16),
        pltpu.VMEM((2, 2, 16, 4, 16, 128), I16),
        pltpu.VMEM((2, 2, 16, 4, 16, 128), I16),
        pltpu.VMEM((2, 2, 4, 1, 128), F32),
        pltpu.VMEM((2, 2, 4, 1, 128), F32),
        pltpu.VMEM((2, 2, 16, 4, 1, 128), F32),
        pltpu.VMEM((2, 2, 8, 2, 64, 128), I16),
        pltpu.VMEM((2, 2, 8, 2, 64, 128), I16),
        pltpu.VMEM((2, 2, 8, 1, 128), F32),
        pltpu.VMEM((2, 2, 8, 1, 128), F32),
        pltpu.VMEM((4, 2, 2, 16, NZ), BF16),
        pltpu.VMEM((16, NZ), I16),
        pltpu.VMEM((4, 16, NZ), I16),
        pltpu.VMEM((2, 64, NZ), F32),
        pltpu.VMEM((2, 64, NZ), F32),
        pltpu.VMEM((2, 768, 256), BF16),
        pltpu.VMEM((2, 256, NZ // 2), BF16),
        pltpu.VMEM((2, 256, NZ // 2), BF16),
        pltpu.VMEM((2, 256, 256), F32),
        dma((8,)),
        dma((2, 2, 4)), dma((2, 2, 4)), dma((2, 2, 16)), dma((2, 2, 16)), dma((2, 2, 8)), dma((2, 2, 8)),
        dma((2, 2, 4)), dma((2, 2, 4)), dma((2, 2, 16)), dma((2, 2, 16)), dma((2, 2, 8)), dma((2, 2, 8)),
        dma((4,)), dma((4,)), dma((4,)), dma((4,)), dma((4,)), dma((4,)), dma,
    ]
    step = pl.pallas_call(
        kernel,
        out_shape=jax.ShapeDtypeStruct((2, 1024, R), F32),
        in_specs=[hbm, hbm, vmem, vmem, hbm, vmem, vmem] + [hbm] * 6,
        out_specs=vmem,
        scratch_shapes=scratch,
        compiler_params=pltpu.CompilerParams(
            collective_id=0, has_side_effects=True, vmem_limit_bytes=56 * 1024 * 1024
        ),
    )
    flat = adj_coef.reshape(2, 1024, R)
    result = step(flat, grid_state, block_index, frozen_depth, inv_blocks, *constants)
    return result.reshape(2, 32, 32, R)


def solution(mesh):
    placed = (
        P(None, "az", "ax", None),
        P(None, "az", "ax", None),
        P("az", "ax"),
        P("ax", None),
        P(),
    )
    return jax.shard_map(
        on_device, mesh=mesh, in_specs=placed, out_specs=P(None, "az", "ax", None), check_vma=False
    )
```

```python
import math

import jax
import jax.numpy as jnp
import ml_dtypes
import numpy as np
from jax import lax
from jax.experimental import pallas as pl
from jax.experimental.pallas import tpu as pltpu
from jax.sharding import PartitionSpec as P

NT = 512
NZ = 1024
R = 128
NB = 8
penalty = 2.0
step_dt = 0.3
QMAX = 32767.0
ROUNDER = 12582912.0
F32 = jnp.float32
BF16 = jnp.bfloat16
I16 = jnp.int16
MESH = pl.DeviceIdType.MESH


def hartley(count):
    index = np.arange(count, dtype=np.int64)
    angle = (index[:, None] * index[None, :] % count) * (2.0 * math.pi / count)
    return (np.cos(angle) + np.sin(angle)) / math.sqrt(count)


def chebyshev(count):
    index = np.arange(count, dtype=np.int64)
    angle = (index[:, None] * index[None, :] % (2 * (count - 1))) * (math.pi / (count - 1))
    return np.cos(angle) * math.sqrt(2.0 / count)


def parts(table):
    high = table.astype(ml_dtypes.bfloat16)
    low = (table - high.astype(np.float64)).astype(ml_dtypes.bfloat16)
    return high, low


def tables():
    q, zl, i = np.meshgrid(np.arange(8), np.arange(2), np.arange(16), indexing="ij")
    theta_order = (16 * (zl * 8 + q) + i).reshape(-1)
    az, half, tg = np.meshgrid(np.arange(16), np.arange(2), np.arange(8), indexing="ij")
    mode_order = (32 * az + tg * 4 + 2 * half).reshape(-1)
    pair, lane = np.meshgrid(np.arange(4), np.arange(128), indexing="ij")
    device = 2 * pair + lane % 2
    axial_order = (32 * (lane // 32 * 8 + device) + lane % 32 // 2 * 2).reshape(-1)
    theta_full = hartley(NT)[theta_order]
    theta = np.stack([theta_full[:, mode_order + par] for par in range(2)])
    axial = np.stack([hartley(NZ)[axial_order + par][:, : NZ // 2] for par in range(2)])
    radial = chebyshev(R)
    ch, cl = parts(radial)
    dh, dl = parts(np.stack([radial[0::2], radial[1::2]]))
    th, tl = parts(theta)
    bh, bl = parts(theta.transpose(0, 2, 1))
    wh, wl = parts(axial)
    vh, vl = parts(np.ascontiguousarray(axial.transpose(0, 2, 1)))
    return [
        np.concatenate([ch, ch, cl], axis=1),
        np.stack([np.concatenate([dh[i], dh[i], dl[i]], axis=0) for i in range(2)]),
        np.concatenate([th, th, tl], axis=2),
        np.concatenate([bh, bh, bl], axis=2),
        wh,
        wl,
        vh,
        vl,
    ]


def split(value):
    high = value.astype(BF16)
    low = (value - high.astype(F32)).astype(BF16)
    return high, low


def dot(a, b, dims=((1,), (0,))):
    return lax.dot_general(a, b, (dims, ((), ())), preferred_element_type=F32)


def swap_groups(tiles):
    lane = lax.broadcasted_iota(jnp.int32, tiles[0].shape, 1)
    first = lane < 64
    even = lane % 64 < 32
    t0, t1, t2, t3 = tiles
    a0 = jnp.where(first, t0, pltpu.roll(t2, 64, 1))
    a2 = jnp.where(first, pltpu.roll(t0, 64, 1), t2)
    a1 = jnp.where(first, t1, pltpu.roll(t3, 64, 1))
    a3 = jnp.where(first, pltpu.roll(t1, 64, 1), t3)
    b0 = jnp.where(even, a0, pltpu.roll(a1, 32, 1))
    b1 = jnp.where(even, pltpu.roll(a0, 96, 1), a1)
    b2 = jnp.where(even, a2, pltpu.roll(a3, 32, 1))
    b3 = jnp.where(even, pltpu.roll(a2, 96, 1), a3)
    return [b0, b1, b2, b3]


def swap_parity(first, second):
    even = lax.broadcasted_iota(jnp.int32, first.shape, 1) % 2 == 0
    return (
        jnp.where(even, first, pltpu.roll(second, 1, 1)),
        jnp.where(even, pltpu.roll(first, 127, 1), second),
    )


def quantize(value, inverse):
    whole = (value * inverse + ROUNDER) - ROUNDER
    return whole.astype(jnp.int32).astype(I16)


def restore(value, scale):
    return value.astype(jnp.int32).astype(F32) * scale


def kernel(
    x_in, st_ref, bi_ref, fd_ref, inv_in, cf_ref, cb_ref,
    tf_in, tb_in, wh_in, wl_in, vh_in, vl_in,
    out_ref,
    x_ref, inv_ref, tf_ref, tb_ref, wh_ref, wl_ref, vh_ref, vl_ref,
    wc_ref, impl_ref, s32_ref, d32_ref,
    s16_ref, xb_ref, zb_ref, sc_ref, xsc_ref, zsc_ref,
    ysend_ref, yrecv_ref, ysc_ref, yscr_ref,
    state_ref, fd16_ref, fdall_ref, keep_ref, tang_ref,
    xcat_ref, a_ref, f_ref, t32_ref,
    table_sem, xs_sem, xr_sem, zs_sem, zr_sem, ys_sem, yr_sem,
    xcs_sem, xcr_sem, zcs_sem, zcr_sem, ycs_sem, ycr_sem,
    us_sem, ur_sem, fs_sem, fr_sem, gs_sem, gr_sem, own_sem,
):
    az = lax.axis_index("az")
    ax = lax.axis_index("ax")
    x = lax.div(az, 4)
    zl = lax.div(ax, 8)
    q = lax.rem(ax, 8)
    y = lax.div(q, 2)
    core = lax.rem(q, 2)
    z = lax.rem(az, 4) * 4 + zl
    group = x * 16 + z

    x_to = [lax.rem(x + k, 4) for k in range(4)]
    z_to = [lax.rem(z + k, 16) for k in range(16)]
    x_home = [(xx * 4 + lax.rem(az, 4), ax) for xx in x_to]
    z_home = [(x * 4 + lax.div(zz, 4), lax.rem(zz, 4) * 8 + q) for zz in z_to]
    y_to = [lax.rem(y + k, 4) for k in range(4)]
    l_to = [lax.rem(zl + k, 4) for k in range(4)]
    l_home = [(az, ll * 8 + q) for ll in l_to]

    def y_home(k, h):
        return (az, zl * 8 + y_to[k] * 2 + h)

    def remote(src, dst, send, recv, device):
        return pltpu.make_async_remote_copy(
            src_ref=src, dst_ref=dst, send_sem=send, recv_sem=recv, device_id=device, device_id_type=MESH
        )

    table_copies = [
        pltpu.make_async_copy(src, dst, table_sem.at[n])
        for n, (src, dst) in enumerate(
            [
                (inv_in, inv_ref), (x_in, x_ref), (tf_in, tf_ref), (tb_in, tb_ref),
                (wh_in, wh_ref), (wl_in, wl_ref), (vh_in, vh_ref), (vl_in, vl_ref),
            ]
        )
    ]
    for copy in table_copies:
        copy.start()
    barrier = pltpu.get_barrier_semaphore()
    homes = x_home[1:] + z_home[1:] + [y_home(k, h) for k in range(1, 4) for h in range(2)] + [y_home(0, 1 - core)]
    for home in homes:
        pl.semaphore_signal(barrier, inc=1, device_id=home, device_id_type=MESH)

    def x_copies(leg, rho, k, to, frm, home):
        data = [
            remote(s16_ref.at[leg, rho, to], xb_ref.at[leg, rho, :, frm], xs_sem.at[leg, rho, k], xr_sem.at[leg, rho, k], home),
        ]
        if leg == 0 and rho == 1:
            return data
        return data + [
            remote(sc_ref.at[leg, rho, to], xsc_ref.at[leg, rho, frm], xcs_sem.at[leg, rho, k], xcr_sem.at[leg, rho, k], home),
        ]

    def z_copies(leg, rho, k, to, frm, home):
        data = [
            remote(xb_ref.at[leg, rho, to], zb_ref.at[leg, rho, frm], zs_sem.at[leg, rho, k], zr_sem.at[leg, rho, k], home),
        ]
        if leg == 0 and rho == 1:
            return data
        return data + [
            remote(xsc_ref.at[leg, rho], zsc_ref.at[leg, rho, frm], zcs_sem.at[leg, rho, k], zcr_sem.at[leg, rho, k], home),
        ]

    def exchange(copies, place, homes, count):
        def start(leg, rho):
            order = (7, 9, 6, 10, 8, 5, 11, 4, 12, 3, 13, 2, 14, 1, 15) if count == 16 else (2, 1, 3)
            for k in order:
                for copy in copies(leg, rho, k, place[k], place[0], homes[k]):
                    copy.start()

        def arrive(leg, rho):
            for k in range(1, count):
                for copy in copies(leg, rho, k, place[0], place[count - k], homes[k]):
                    copy.wait_recv()

        def sent(leg, rho):
            for k in range(1, count):
                for copy in copies(leg, rho, k, place[k], place[0], homes[k]):
                    copy.wait_send()

        return start, arrive, sent

    _, x_arrive, x_sent = exchange(x_copies, x_to, x_home, 4)
    z_start, z_arrive, z_sent = exchange(z_copies, z_to, z_home, 16)

    def y_copies(leg, rho, k, h, frm, frm_core):
        to = y_to[k] * 2 + h
        send = 2 * k + h
        recv = 2 * k + frm_core
        return [
            remote(ysend_ref.at[leg, rho, to], yrecv_ref.at[leg, rho, frm], ys_sem.at[leg, rho, send], yr_sem.at[leg, rho, recv], y_home(k, h)),
            remote(ysc_ref.at[leg, rho, to], yscr_ref.at[leg, rho, frm], ycs_sem.at[leg, rho, send], ycr_sem.at[leg, rho, recv], y_home(k, h)),
        ]

    def y_partners(k):
        return (0, 1) if k else (1 - core,)

    def y_send(leg, rho, k):
        for h in y_partners(k):
            for copy in y_copies(leg, rho, k, h, q, core):
                copy.start()
        if k == 0:
            yrecv_ref[leg, rho, q] = ysend_ref[leg, rho, q]
            yscr_ref[leg, rho, q] = ysc_ref[leg, rho, q]

    def y_arrive(leg, rho):
        for k in (2, 1, 3, 0):
            for h in y_partners(k):
                for copy in y_copies(leg, rho, k, core, y_to[(4 - k) % 4] * 2 + h, h):
                    copy.wait_recv()

    def y_sent(leg, rho):
        for k in range(4):
            for h in y_partners(k):
                for copy in y_copies(leg, rho, k, h, q, core):
                    copy.wait_send()

    def x_send(leg, rho, k):
        if k:
            for copy in x_copies(leg, rho, k, x_to[k], x, x_home[k]):
                copy.start()
        else:
            xb_ref[leg, rho, :, x] = s16_ref[leg, rho, x]
            if leg == 1 or rho == 0:
                xsc_ref[leg, rho, x] = sc_ref[leg, rho, x]

    def z_phase(leg, rho):
        x_arrive(leg, rho)
        z_start(leg, rho)
        zb_ref[leg, rho, z] = xb_ref[leg, rho, z]
        if leg == 1 or rho == 0:
            zsc_ref[leg, rho, z] = xsc_ref[leg, rho]

    def operators(f):
        for b in range(NB):
            high, low = split(inv_ref[b, f].T)
            columns = slice(b % 2 * 128, b % 2 * 128 + 128)
            wc_ref[f, b // 2, 0:128, columns] = high
            wc_ref[f, b // 2, 128:256, columns] = high
            wc_ref[f, b // 2, 256:384, columns] = low

    def radial_forward(f):
        eye = lax.broadcasted_iota(jnp.int32, (32, 32), 0) == lax.broadcasted_iota(jnp.int32, (32, 32), 1)
        ones = jnp.ones((32, 128), BF16)
        largest = jnp.zeros((4, 128), F32)
        for rt in range(4):
            rows = slice(rt * 256, rt * 256 + 256)
            labels = bi_ref[rt * 8 : rt * 8 + 8, :].astype(F32)
            spread = [jnp.where(eye, jnp.broadcast_to(labels[t : t + 1], (32, 32)), 0.0) for t in range(8)]
            label = dot(jnp.concatenate(spread, axis=0).astype(BF16), ones)
            high, low = split(x_ref[f, rows, :])
            both = jnp.concatenate([high, low, high], axis=1)
            total = jnp.zeros((256, 128), F32)
            for b in range(0, NB, 2):
                pair = dot(both, wc_ref[f, b // 2])
                total = jnp.where(label == float(b), pair[:, :128], total)
                total = jnp.where(label == float(b + 1), pair[:, 128:], total)
            impl_ref[f, rows, :] = total
            high, low = split(total)
            grid = dot(cf_ref[...], jnp.concatenate([high, low, high], axis=1), ((1,), (1,)))
            for h in range(2):
                piece = grid[:, h * 128 : h * 128 + 128]
                s32_ref[f, pl.ds(rt * 2 + h, 128, stride=8), :] = piece
                largest = jnp.maximum(largest, jnp.max(jnp.abs(piece).reshape(4, 32, 128), axis=1))
        return largest

    for f in range(2):
        table_copies[f].wait()
    operators(0)
    operators(1)
    largest = jnp.maximum(jnp.maximum(radial_forward(0), radial_forward(1)), 1e-30)
    inverse = QMAX / largest
    scale = largest * (1.0 / QMAX)
    for xx in range(4):
        sc_ref[0, 0, xx] = scale[xx : xx + 1]

    def code(rho):
        for xx in range(4):
            both = [
                s32_ref[f, xx * 256 : xx * 256 + 256, :].reshape(16, 2, 8, 128)[:, rho] for f in range(2)
            ]
            s16_ref[0, rho, xx] = quantize(jnp.concatenate(both, axis=1), inverse[xx : xx + 1])

    code(0)

    pl.semaphore_wait(barrier, 25)
    for k in (2, 1, 3, 0):
        x_send(0, 0, k)
    code(1)
    for k in (2, 1, 3, 0):
        x_send(0, 1, k)

    fd16_ref[...] = fd_ref[...].astype(I16)
    quarter = pl.ds(pl.multiple_of(x * 256, 256), 256)

    def state_copy(k, to, frm):
        return remote(st_ref.at[:, pl.ds(2 * to, 2)], state_ref.at[frm], us_sem.at[k], ur_sem.at[k], l_home[k])

    def quarter_copy(k, frm):
        return remote(fd16_ref.at[:, quarter], fdall_ref.at[frm, :, quarter], fs_sem.at[k], fr_sem.at[k], l_home[k])

    def depth_copy(k, frm):
        part = pl.ds(pl.multiple_of(frm * 256, 256), 256)
        return remote(fdall_ref.at[:, :, part], fdall_ref.at[:, :, part], gs_sem.at[k], gr_sem.at[k], x_home[k])

    own_state = pltpu.make_async_copy(st_ref.at[:, pl.ds(2 * zl, 2)], state_ref.at[zl], own_sem)
    own_state.start()
    fdall_ref[zl, :, quarter] = fd16_ref[:, quarter]
    z_phase(0, 0)
    for k in (2, 1, 3):
        quarter_copy(k, zl).start()
        state_copy(k, l_to[k], zl).start()
    z_phase(0, 1)

    for copy in table_copies[2:]:
        copy.wait()

    def keep_columns(par, rows, f, value):
        high, low = split(value)
        start, size = rows
        columns = slice(f * 128, f * 128 + 128)
        xcat_ref[par, pl.ds(start, size), columns] = high
        xcat_ref[par, pl.ds(256 + start, size), columns] = low
        xcat_ref[par, pl.ds(512 + start, size), columns] = high

    def send_block(leg, rho, p, fields):
        most = jnp.maximum(jnp.abs(fields[0]), jnp.abs(fields[1]))
        most = jnp.maximum(jnp.max(most, axis=0, keepdims=True), 1e-30)
        inverse = QMAX / most
        ysc_ref[leg, rho, p] = most * (1.0 / QMAX)
        for f in range(2):
            ysend_ref[leg, rho, p, f] = quantize(fields[f], inverse)

    def theta_forward(rho):
        z_arrive(0, rho)

        def body(xx, carry):
            for zh in range(4):
                tiles = [
                    restore(zb_ref[0, rho, zh * 4 + s, xx], zsc_ref[0, 0, zh * 4 + s, xx]) for s in range(4)
                ]
                tiles = swap_groups(tiles)
                start = pl.multiple_of(xx * 64 + zh * 16, 16)
                for f in range(2):
                    for par in range(2):
                        rows = jnp.concatenate([tile[f * 8 : f * 8 + 8] for tile in tiles[par::2]], axis=0)
                        keep_columns(par, (start, 16), f, rows)
            return carry

        lax.fori_loop(0, 4, body, 0)
        evens = dot(tf_ref[0], xcat_ref[0])
        odds = dot(tf_ref[1], xcat_ref[1])
        t32_ref[0] = evens + odds
        t32_ref[1] = evens - odds
        for k in (2, 1, 3, 0):
            for h in range(2):
                p = y_to[k] * 2 + h
                rows = pl.ds(pl.multiple_of(p * 32, 32), 32)
                grid = jnp.concatenate([t32_ref[0, rows, :], t32_ref[1, rows, :]], axis=0)
                send_block(0, rho, p, [grid[:, f * 128 : f * 128 + 128] for f in range(2)])
            y_send(0, rho, k)

    def axial_forward(rho):
        y_arrive(0, rho)
        for m in range(4):
            lanes = slice(m * 128, m * 128 + 128)
            for f in range(2):
                pair = swap_parity(*[restore(yrecv_ref[0, rho, p, f], yscr_ref[0, rho, p]) for p in (2 * m, 2 * m + 1)])
                for par in range(2):
                    high, low = split(pair[par])
                    a_ref[par, f * 64 : f * 64 + 64, lanes] = high
                    a_ref[par, 128 + f * 64 : 128 + f * 64 + 64, lanes] = low

        def force(grid, columns):
            keep = keep_ref[rho, :, columns]
            u0 = jnp.concatenate([state_ref[s, 0, rho, :, columns] for s in range(4)], axis=0).astype(F32)
            u1 = jnp.concatenate([state_ref[s, 1, rho, :, columns] for s in range(4)], axis=0).astype(F32)
            g0 = grid[:64]
            g1 = grid[64:]
            pull = tang_ref[rho, :, columns] * (u0 * g0 + u1 * g1)
            return jnp.concatenate([pull * u0 - keep * g0, pull * u1 - keep * g1], axis=0)

        for n in range(2):
            columns = slice(n * 256, n * 256 + 256)
            sums = []
            for par in range(2):
                twice = dot(a_ref[par], wh_ref[par, :, columns])
                sums.append(twice[:128] + twice[128:] + dot(a_ref[par, :128], wl_ref[par, :, columns]))
            lower = force(sums[0] + sums[1], columns)
            upper = force(sums[0] - sums[1], slice(512 + n * 256, 512 + n * 256 + 256))
            for par, value in enumerate((lower + upper, lower - upper)):
                high, low = split(value)
                f_ref[par, :128, columns] = high
                f_ref[par, 128:, columns] = low

    def axial_back(rho):
        own_half = lax.div(y, 2)
        for i in range(2):
            n = own_half if i else 1 - own_half
            columns = pl.ds(pl.multiple_of(n * 256, 256), 256)
            modes = []
            for par in range(2):
                twice = dot(f_ref[par], vh_ref[par, :, columns])
                modes.append(twice[:128] + twice[128:] + dot(f_ref[par, :128], vl_ref[par, :, columns]))
            for m in range(2):
                lanes = slice(m * 128, m * 128 + 128)
                blocks = swap_parity(modes[0][:, lanes], modes[1][:, lanes])
                for h in range(2):
                    send_block(1, rho, n * 4 + m * 2 + h, [blocks[h][f * 64 : f * 64 + 64] for f in range(2)])
            for k in (1, 3, 0) if i else (2,):
                y_send(1, rho, k)

    def theta_back(rho):
        y_arrive(1, rho)
        for p in range(8):
            for f in range(2):
                grid = restore(yrecv_ref[1, rho, p, f], yscr_ref[1, rho, p])
                keep_columns(0, (p * 32, 32), f, grid[:32] + grid[32:])
                keep_columns(1, (p * 32, 32), f, grid[:32] - grid[32:])
        for par in range(2):
            t32_ref[par] = dot(tb_ref[par], xcat_ref[par])
        for k in (2, 1, 3, 0):
            xx = x_to[k]
            rows = pl.ds(pl.multiple_of(xx * 64, 64), 64)
            modes = [t32_ref[par, rows, :] for par in range(2)]
            tiles = []
            for n in range(4):
                tiles += swap_groups([
                    jnp.concatenate(
                        [
                            modes[a % 2][n * 16 + a // 2 * 8 : n * 16 + a // 2 * 8 + 8, f * 128 : f * 128 + 128]
                            for f in range(2)
                        ],
                        axis=0,
                    )
                    for a in range(4)
                ])
            most = jnp.abs(tiles[0])
            for tile in tiles[1:]:
                most = jnp.maximum(most, jnp.abs(tile))
            most = jnp.maximum(jnp.max(most, axis=0, keepdims=True), 1e-30)
            inverse = QMAX / most
            sc_ref[1, rho, xx] = most * (1.0 / QMAX)
            for n in range(16):
                s16_ref[1, rho, xx, n] = quantize(tiles[n], inverse)
            x_send(1, rho, k)

    theta_forward(0)

    for k in range(1, 4):
        quarter_copy(k, l_to[4 - k]).wait_recv()
    for k in range(1, 4):
        depth_copy(k, x).start()

    for k in range(1, 4):
        state_copy(k, zl, l_to[4 - k]).wait_recv()
        depth_copy(k, x_to[4 - k]).wait_recv()
    own_state.wait()
    for rho in range(2):
        for s in range(4):
            u0 = state_ref[s, 0, rho].astype(F32)
            u1 = state_ref[s, 1, rho].astype(F32)
            root = lax.rsqrt(1.0 + (u0 * u0 + u1 * u1))
            viscosity = root * lax.rsqrt(root)
            depth = fdall_ref[s].astype(jnp.int32)
            frozen = jnp.where(2 * group + rho >= R - depth, penalty, 0.0)
            keep_ref[rho, s * 16 : s * 16 + 16] = viscosity + frozen
            tang_ref[rho, s * 16 : s * 16 + 16] = 0.5 * viscosity * (root * root)

    axial_forward(0)
    axial_back(0)
    theta_forward(1)
    theta_back(0)
    axial_forward(1)
    axial_back(1)
    z_phase(1, 0)
    theta_back(1)
    z_phase(1, 1)

    for leg, rho in ((0, 0), (0, 1), (1, 0)):
        x_sent(leg, rho)
        z_sent(leg, rho)
        y_sent(leg, rho)
    x_sent(1, 1)
    y_sent(1, 1)
    for k in range(1, 4):
        state_copy(k, l_to[k], zl).wait_send()
        quarter_copy(k, zl).wait_send()
        depth_copy(k, x).wait_send()
    for rho in range(2):
        z_arrive(1, rho)
        for xx in range(4):
            tile = restore(zb_ref[1, rho, :, xx], zsc_ref[1, rho, :, xx])
            for f in range(2):
                d32_ref[f, xx * 128 : xx * 128 + 128, :] = tile[:, f * 8 : f * 8 + 8].reshape(128, 128)
        for f in range(2):
            for tg in range(8):
                high, low = split(d32_ref[f, pl.ds(tg, 64, stride=8), :])
                gamma = dot(jnp.concatenate([high, low, high], axis=0), cb_ref[rho], ((0,), (0,)))
                rows = slice(tg * 128, tg * 128 + 128)
                before = impl_ref if rho == 0 else out_ref
                out_ref[f, rows, :] = before[f, rows, :] + step_dt * gamma
    z_sent(1, 1)


def on_device(adj_coef, grid_state, block_index, frozen_depth, inv_blocks):
    constants = [jnp.asarray(table) for table in tables()]
    vmem = pl.BlockSpec(memory_space=pltpu.VMEM)
    hbm = pl.BlockSpec(memory_space=pltpu.HBM)
    dma = pltpu.SemaphoreType.DMA
    scratch = [
        pltpu.VMEM((2, 1024, 128), F32),
        pltpu.VMEM((NB, 2, 128, 128), F32),
        pltpu.VMEM((2, 256, 768), BF16),
        pltpu.VMEM((2, 256, 768), BF16),
        pltpu.VMEM((2, NZ // 2, NZ // 2), BF16),
        pltpu.VMEM((2, NZ // 2, NZ // 2), BF16),
        pltpu.VMEM((2, NZ // 2, NZ // 2), BF16),
        pltpu.VMEM((2, NZ // 2, NZ // 2), BF16),
        pltpu.VMEM((2, NB // 2, 384, 256), BF16),
        pltpu.VMEM((2, 1024, 128), F32),
        pltpu.VMEM((2, 1024, 128), F32),
        pltpu.VMEM((2, 512, 128), F32),
        pltpu.VMEM((2, 2, 4, 16, 16, 128), I16),
        pltpu.VMEM((2, 2, 16, 4, 16, 128), I16),
        pltpu.VMEM((2, 2, 16, 4, 16, 128), I16),
        pltpu.VMEM((2, 2, 4, 1, 128), F32),
        pltpu.VMEM((2, 2, 4, 1, 128), F32),
        pltpu.VMEM((2, 2, 16, 4, 1, 128), F32),
        pltpu.VMEM((2, 2, 8, 2, 64, 128), I16),
        pltpu.VMEM((2, 2, 8, 2, 64, 128), I16),
        pltpu.VMEM((2, 2, 8, 1, 128), F32),
        pltpu.VMEM((2, 2, 8, 1, 128), F32),
        pltpu.VMEM((4, 2, 2, 16, NZ), BF16),
        pltpu.VMEM((16, NZ), I16),
        pltpu.VMEM((4, 16, NZ), I16),
        pltpu.VMEM((2, 64, NZ), F32),
        pltpu.VMEM((2, 64, NZ), F32),
        pltpu.VMEM((2, 768, 256), BF16),
        pltpu.VMEM((2, 256, NZ // 2), BF16),
        pltpu.VMEM((2, 256, NZ // 2), BF16),
        pltpu.VMEM((2, 256, 256), F32),
        dma((8,)),
        dma((2, 2, 4)), dma((2, 2, 4)), dma((2, 2, 16)), dma((2, 2, 16)), dma((2, 2, 8)), dma((2, 2, 8)),
        dma((2, 2, 4)), dma((2, 2, 4)), dma((2, 2, 16)), dma((2, 2, 16)), dma((2, 2, 8)), dma((2, 2, 8)),
        dma((4,)), dma((4,)), dma((4,)), dma((4,)), dma((4,)), dma((4,)), dma,
    ]
    step = pl.pallas_call(
        kernel,
        out_shape=jax.ShapeDtypeStruct((2, 1024, R), F32),
        in_specs=[hbm, hbm, vmem, vmem, hbm, vmem, vmem] + [hbm] * 6,
        out_specs=vmem,
        scratch_shapes=scratch,
        compiler_params=pltpu.CompilerParams(
            collective_id=0, has_side_effects=True, vmem_limit_bytes=56 * 1024 * 1024
        ),
    )
    flat = adj_coef.reshape(2, 1024, R)
    result = step(flat, grid_state, block_index, frozen_depth, inv_blocks, *constants)
    return result.reshape(2, 32, 32, R)


def solution(mesh):
    placed = (
        P(None, "az", "ax", None),
        P(None, "az", "ax", None),
        P("az", "ax"),
        P("ax", None),
        P(),
    )
    return jax.shard_map(
        on_device, mesh=mesh, in_specs=placed, out_specs=P(None, "az", "ax", None), check_vma=False
    )
```
